256 devices in a mesh: wide: 64 (over y, x_lo, z), narrow: 4 (over x_hi, core).
Axes of the slice: x: 4 (x_hi: 2, x_lo: 2; x = x_hi * 2 + x_lo), y: 4, z: 8, core: 2. Of those that a mesh axis runs over, the one named last changes fastest.
Arguments:
- displacement: float32 [3, 8, 512, 512], P(None, None, 'wide', 'narrow'), may hold values from -6 to 6
- lift_weight: float32 [3, 64], replicated, may hold values from -5 to 5
- conv1_weight: bfloat16 [3, 3, 3, 64, 64], replicated, may hold values from -0.21875 to 0.21875
- first_reduce_weight: bfloat16 [2, 2, 2, 64, 128], replicated, may hold values from -0.375 to 0.375
- conv2_weight: bfloat16 [3, 3, 3, 128, 128], replicated, may hold values from -0.15625 to 0.15625
- second_reduce_weight: bfloat16 [2, 2, 2, 128, 256], replicated, may hold values from -0.25 to 0.25
- conv3_weight: bfloat16 [3, 3, 3, 256, 256], replicated, may hold values from -0.109375 to 0.109375
Outputs:
- finest_skip_features: bfloat16 [64, 8, 512, 512], P(None, None, 'wide', 'narrow')
- middle_skip_features: bfloat16 [128, 4, 256, 256], P(None, None, 'wide', 'narrow')
- coarse_features: bfloat16 [256, 2, 128, 128], P('wide', None, None, 'narrow')
The draws below stay inside these ranges and needn't reach their ends.
All inputs are finite; a program needn't handle non-finite values.
Results may differ from the reference program's by a relative error of at most 0.013.
Values may be sent and summed in bfloat16 or wider, within the bound.
No kernel may reach another device: no remote copies, remote signals or barrier semaphores. Data moves between devices by JAX's collectives and lax.ppermute only.
A program may use at most 128 MiB of HBM per device.

```python
import jax
import jax.numpy as jnp
from jax import lax

C_IN = 3
C1 = 64
C2 = 128
C3 = 256
DEPTH = 8
NY = 512
NX = 512


def steps_of(rng, extent, cuts, least, high):
    gain = 1.0
    for axis_at, blocks in cuts:
        draws = jax.random.uniform(jax.random.fold_in(jax.random.fold_in(rng, 6), axis_at), (blocks,), jnp.float32, least / len(cuts), high / len(cuts))
        gain = gain * jnp.repeat(jnp.exp(draws), extent[axis_at] // blocks).reshape((-1,) + (1,) * (len(extent) - 1 - axis_at))
    return gain


def scatter_about(own_key, shape, scale, bound, pieces=(), dtype=jnp.bfloat16):
    drawn = scale * jax.random.normal(own_key, shape, jnp.float32)
    if pieces:
        drawn = drawn * steps_of(own_key, shape, pieces, -0.22, 0.18)
    return jnp.clip(drawn, -bound, bound).astype(dtype)


def setup_inputs(seed: int = 0) -> dict:
    streams_of = jax.random.split(jax.random.key(seed), 8)
    return {
        "displacement": scatter_about(streams_of[0], (C_IN, DEPTH, NY, NX), 1.0, 6.0, ((2, 64), (3, 4)), jnp.float32),
        "lift_weight": scatter_about(streams_of[1], (C_IN, C1), 1.5 ** -0.5, 5.0, (), jnp.float32),
        "conv1_weight": scatter_about(streams_of[2], (3, 3, 3, C1, C1), (27 * C1 // 2) ** -0.5, 0.21875),
        "first_reduce_weight": scatter_about(streams_of[3], (2, 2, 2, C1, C2), (4 * C1) ** -0.5, 0.375),
        "conv2_weight": scatter_about(streams_of[4], (3, 3, 3, C2, C2), (27 * C2 // 2) ** -0.5, 0.15625),
        "second_reduce_weight": scatter_about(streams_of[5], (2, 2, 2, C2, C3), (4 * C2) ** -0.5, 0.25),
        "conv3_weight": scatter_about(streams_of[6], (3, 3, 3, C3, C3), (27 * C3 // 2) ** -0.5, 0.109375),
    }


def leaky_rectifier(values):
    return jnp.maximum(values, 0.01 * values)


def convolve(displacement_grid, filter_weight):
    padded = jnp.pad(displacement_grid.astype(jnp.float32), ((0, 0), (0, 0), (1, 1), (1, 1)), mode="wrap")
    result = lax.conv_general_dilated(padded[None], filter_weight.astype(jnp.float32), (1, 1, 1), ((1, 1), (0, 0), (0, 0)), dimension_numbers=("NCDHW", "DHWIO", "NCDHW"), precision=lax.Precision.HIGHEST)
    return result[0]


def strided_reduce(displacement_grid, filter_weight):
    result = lax.conv_general_dilated(displacement_grid.astype(jnp.float32)[None], filter_weight.astype(jnp.float32), (2, 2, 2), "VALID", dimension_numbers=("NCDHW", "DHWIO", "NCDHW"), precision=lax.Precision.HIGHEST)
    return result[0]


def reference(displacement, lift_weight, conv1_weight, first_reduce_weight, conv2_weight, second_reduce_weight, conv3_weight):
    lifted = jnp.einsum("mo,mzyx->ozyx", lift_weight, displacement, precision=lax.Precision.HIGHEST)
    lifted = leaky_rectifier(lifted).astype(jnp.bfloat16)
    finest_skip_features = leaky_rectifier(convolve(lifted, conv1_weight)).astype(jnp.bfloat16)
    middle_level = leaky_rectifier(strided_reduce(finest_skip_features, first_reduce_weight)).astype(jnp.bfloat16)
    middle_skip_features = leaky_rectifier(convolve(middle_level, conv2_weight)).astype(jnp.bfloat16)
    coarsest_level = leaky_rectifier(strided_reduce(middle_skip_features, second_reduce_weight)).astype(jnp.bfloat16)
    coarse_features = leaky_rectifier(convolve(coarsest_level, conv3_weight)).astype(jnp.bfloat16)
    return finest_skip_features, middle_skip_features, coarse_features
```

```python
import jax
import jax.numpy as jnp
from jax import lax
from jax.experimental import pallas as pl
from jax.experimental.pallas import tpu as pltpu
from jax.sharding import PartitionSpec as P

F32 = jnp.float32
BF = jnp.bfloat16
VMEM = pltpu.VMEM
LIMIT = 58 * 1024 * 1024


def leaky(v):
    return jnp.maximum(v, 0.01 * v)


def rounded(v):
    return v.astype(BF).astype(F32)


def mm(a, b):
    return jnp.dot(a, b, preferred_element_type=F32)


def call(kernel, outs, args, scratch=(), name=None, flops=0, nbytes=0, in_specs=None):
    whole = pl.BlockSpec(memory_space=VMEM)
    return pl.pallas_call(
        kernel,
        out_shape=outs,
        in_specs=[whole] * len(args) if in_specs is None else in_specs,
        out_specs=jax.tree.map(lambda _: whole, outs),
        scratch_shapes=list(scratch),
        compiler_params=pltpu.CompilerParams(vmem_limit_bytes=LIMIT),
        cost_estimate=pl.CostEstimate(flops=flops, bytes_accessed=nbytes, transcendentals=0),
        name=name,
    )(*args)


def weights_kernel(lift_ref, c1_ref, c2_ref, wl_ref, w1_ref, w2_ref):
    w = lift_ref[...]
    hi = rounded(w)
    low = rounded(w - hi)
    place = (
        lax.broadcasted_iota(jnp.int32, (64, 256), 1) % 64
        == lax.broadcasted_iota(jnp.int32, (64, 256), 0)
    ).astype(BF)
    hi4 = mm(hi.astype(BF), place)
    low4 = mm(low.astype(BF), place)
    terms = []
    for s in range(5):
        for m in range(3):
            src = low4 if s in (1, 3) else hi4
            terms.append(jnp.broadcast_to(src[m : m + 1, :], (8, 256)))
    terms.append(jnp.zeros((8, 256), F32))
    base = jnp.concatenate(terms, axis=0)
    row = lax.broadcasted_iota(jnp.int32, (128, 256), 0) % 8
    column = lax.broadcasted_iota(jnp.int32, (128, 256), 1) // 64
    for i in range(8):
        for j in range(4):
            keep = (row == i) & (column == j)
            wl_ref[i, j * 128 : (j + 1) * 128, :] = jnp.where(keep, base, 0.0).astype(BF)
    rows64 = lax.broadcasted_iota(jnp.int32, (64, 128), 0)
    lanes64 = lax.broadcasted_iota(jnp.int32, (64, 128), 1)
    left = (rows64 == lanes64).astype(BF)
    right = (rows64 + 64 == lanes64).astype(BF)
    zero1 = jnp.zeros((256, 128), BF)
    zero64 = jnp.zeros((64, 128), F32)
    for b in range(3):
        for a in range(3):
            k = c1_ref[a * 3 + b]
            pair = jnp.concatenate([mm(k, left), zero64], 0) + jnp.concatenate(
                [zero64, mm(k, right)], 0
            )
            pair = pair.astype(BF)
            w1_ref[a * 3 + b, :, 0:128] = pair
            w1_ref[(a + 1) * 3 + b, :, 128:256] = pair
        w1_ref[9 + b, :, 0:128] = zero1
        w1_ref[b, :, 128:256] = zero1
    zero2 = jnp.zeros((384, 128), BF)
    for b in range(3):
        for a in range(3):
            w2_ref[a * 3 + b, :, 0:128] = c2_ref[a * 3 + b]
            w2_ref[(a + 1) * 3 + b, :, 128:256] = c2_ref[a * 3 + b]
        w2_ref[9 + b, :, 0:128] = zero2
        w2_ref[b, :, 128:256] = zero2


def turn_kernel(up_ref, own_ref, down_ref, dt_ref, left_ref, right_ref):
    for plane in range(8):
        for blk, src in enumerate((up_ref, own_ref, down_ref)):
            parts = [[], [], []]
            for m in range(3):
                v = src[m * 8 + plane]
                hi = rounded(v)
                rest = v - hi
                mid = rounded(rest)
                parts[0].append(hi)
                parts[1].append(mid)
                parts[2].append(rest - mid)
            tiles = parts[0] + parts[0] + parts[1] + parts[1] + parts[2]
            tiles.append(jnp.zeros((8, 128), F32))
            turned = jnp.concatenate(tiles, axis=0).T
            g = plane * 3 + blk
            dt_ref[g, 8:136] = turned
            left_ref[g] = turned[0:8]
            right_ref[g] = turned[120:128]
    dt_ref[:, 0:8, :] = jnp.zeros((24, 8, 128), F32)
    dt_ref[:, 136:144, :] = jnp.zeros((24, 8, 128), F32)


def fine_levels(lhs_ref, wl_ref, w1_ref, wr1_ref, x4_ref, fn_ref, mid_ref, pairs, chunk):
    zero = jnp.zeros((24, pairs, 256), BF)
    x4_ref[0] = zero
    x4_ref[9] = zero

    def lift(i, carry):
        out = leaky(mm(lhs_ref[...], wl_ref[i])).astype(BF)
        for g in range(24):
            x4_ref[1 + g // 3, (g % 3) * 8 + i] = out[g * pairs : (g + 1) * pairs]
        return carry

    lax.fori_loop(0, 8, lift, 0)
    weight = w1_ref[...].reshape(3072, 256)

    def conv(pp, carry):
        for r0 in range(0, 20, chunk):
            lhs = jnp.concatenate(
                [
                    x4_ref[2 * pp + dp, 1 + b + r0 : 1 + b + r0 + chunk].reshape(
                        chunk * pairs, 256
                    )
                    for dp in range(4)
                    for b in range(3)
                ],
                axis=1,
            )
            out = leaky(mm(lhs, weight)).astype(BF)
            for q in range(2):
                fn_ref[2 * pp + q, r0 // 2 : (r0 + chunk) // 2] = out[
                    :, q * 128 : (q + 1) * 128
                ].reshape(chunk // 2, 2, pairs, 128)
        lhs = jnp.concatenate(
            [
                fn_ref[2 * pp + a, :, b].reshape(10 * pairs, 128)
                for a in range(2)
                for b in range(2)
            ],
            axis=1,
        )
        out = leaky(mm(lhs, wr1_ref[...]))
        mid_ref[pp] = out.astype(mid_ref.dtype).reshape(10, pairs, 128)
        return carry

    lax.fori_loop(0, 4, conv, 0)


def inner_kernel(dt_ref, wl_ref, w1_ref, wr1_ref, fin_ref, mid_ref, lhs_ref, x4_ref, fn_ref):
    def gather(g, carry):
        lhs_ref[pl.ds(pl.multiple_of(g * 64, 64), 64), :] = jnp.concatenate(
            [dt_ref[g, pl.ds(7 + j, 64, stride=2)] for j in range(4)], axis=1
        ).astype(BF)
        return carry

    lax.fori_loop(0, 24, gather, 0)
    fine_levels(lhs_ref, wl_ref, w1_ref, wr1_ref, x4_ref, fn_ref, mid_ref, 64, 10)
    for plane in range(8):
        fin_ref[plane] = fn_ref[plane, 3:7].reshape(8, 64, 128)


def outer_kernel(
    lrecv_ref, left_ref, right_ref, rrecv_ref, wl_ref, w1_ref, wr1_ref, main_ref, w2_hbm, wr2_hbm, w3_hbm,
    edge_ref, skip_ref, chunk_ref,
    de_ref, lhs_ref, x4_ref, fn_ref, me_ref, mf_ref, xm_ref, ms_ref, cf_ref, w2_ref, wr2_ref, w3_ref, sems,
):
    copies = [
        pltpu.make_async_copy(src, dst, sems.at[n])
        for n, (src, dst) in enumerate(((w2_hbm, w2_ref), (wr2_hbm, wr2_ref), (w3_hbm, w3_ref)))
    ]
    for copy in copies:
        copy.start()
    de_ref[:, 0:8] = lrecv_ref[...]
    de_ref[:, 8:16] = left_ref[...]
    de_ref[:, 16:24] = right_ref[...]
    de_ref[:, 24:32] = rrecv_ref[...]
    de_ref[:, 32:40] = jnp.zeros((24, 8, 128), F32)
    for g in range(24):
        lhs_ref[g * 16 : (g + 1) * 16, :] = jnp.concatenate(
            [
                jnp.concatenate(
                    [
                        de_ref[g, pl.ds(1 + j, 8, stride=2)],
                        de_ref[g, pl.ds(21 + j, 8, stride=2)],
                    ],
                    axis=0,
                )
                for j in range(4)
            ],
            axis=1,
        ).astype(BF)
    fine_levels(lhs_ref, wl_ref, w1_ref, wr1_ref, x4_ref, fn_ref, me_ref, 16, 20)
    for plane in range(8):
        edge_ref[plane] = fn_ref[plane, 3:7].reshape(8, 16, 128)

    def merge(n, carry):
        plane, row = n // 10, n % 10
        mf_ref[n, 3:67] = main_ref[plane, row].astype(F32)
        mf_ref[n, 0:4] = me_ref[plane, row, 0:4]
        mf_ref[n, 66:70] = me_ref[plane, row, 8:12]
        for c in range(3):
            xm_ref[plane, row, :, c * 128 : (c + 1) * 128] = mf_ref[n, c : c + 80].astype(BF)
        return carry

    lax.fori_loop(0, 40, merge, 0)
    copies[0].wait()
    for half in range(2):
        taps = range(1, 4) if half == 0 else range(0, 3)
        lhs = jnp.concatenate(
            [
                xm_ref[2 * half - 1 + dp, b : b + 8].reshape(640, 384)
                for dp in taps
                for b in range(3)
            ],
            axis=1,
        )
        weight = w2_ref[taps[0] * 3 : taps[0] * 3 + 9].reshape(3456, 256)
        out = rounded(leaky(mm(lhs, weight)))
        for q in range(2):
            ms_ref[2 * half + q] = out[:, q * 128 : (q + 1) * 128].reshape(8, 80, 128)
    for plane in range(4):
        for row in range(4):
            skip_ref[plane, row] = ms_ref[plane, row + 2, 2:66].astype(BF)
    copies[1].wait()
    taps = []
    for a in range(2):
        for b in range(2):
            for c in range(2):
                taps.append(
                    jnp.concatenate(
                        [
                            ms_ref[2 * plane + a, 2 * row + b, pl.ds(c, 40, stride=2)]
                            for plane in range(2)
                            for row in range(4)
                        ],
                        axis=0,
                    )
                )
    lhs = jnp.concatenate(taps, axis=1).astype(BF)
    out = rounded(leaky(mm(lhs, wr2_ref[...])))
    cf_ref[...] = out.reshape(2, 4, 40, 256)
    lhs = []
    for plane in range(2):
        lhs.append(
            jnp.concatenate(
                [
                    jnp.concatenate(
                        [cf_ref[plane, row + b, c : c + 32] for row in range(2)], axis=0
                    )
                    for b in range(3)
                    for c in range(3)
                ],
                axis=1,
            ).astype(BF)
        )
    copies[2].wait()
    same = mm(jnp.concatenate(lhs, axis=0), w3_ref[1])
    first = same[0:64] + mm(lhs[1], w3_ref[2])
    second = same[64:128] + mm(lhs[0], w3_ref[0])
    out = jnp.concatenate([first[0:32], second[0:32], first[32:64], second[32:64]], axis=0)
    out = leaky(out).T
    chunk_ref[...] = out.reshape(64, 4, 128)


def finest_kernel(fin_ref, edge_ref, out_ref, wide_ref, tile_ref):
    lane = lax.broadcasted_iota(jnp.int32, (64, 128), 1)
    for row in range(0, 8, 2):
        now = []
        for r in (row, row + 1):
            tile_ref[...] = fin_ref[0, r].astype(F32)
            tile_ref[0:1] = edge_ref[0, r, 3:4].astype(F32)
            tile_ref[63:64] = edge_ref[0, r, 8:9].astype(F32)
            now.append(tile_ref[...])
        even = jnp.where(lane < 64, now[0], pltpu.roll(now[1], 64, 1))
        odd = jnp.where(lane < 64, pltpu.roll(now[0], 64, 1), now[1])
        wide_ref[pl.ds(0, 64, stride=2), :] = even
        wide_ref[pl.ds(1, 64, stride=2), :] = odd
        turned = wide_ref[...].T
        out_ref[:, 0, row, :] = turned[0:64].astype(out_ref.dtype)
        out_ref[:, 0, row + 1, :] = turned[64:128].astype(out_ref.dtype)


def coarse_kernel(in_ref, out_ref, y_ref):
    for c in range(4):
        v = in_ref[:, c, :]
        y_ref[pl.ds(0, 64, stride=2), :] = v
        y_ref[pl.ds(1, 64, stride=2), :] = pltpu.roll(v, 64, 1)
        out_ref[c] = y_ref[...].T[0:64].reshape(2, 32, 128).astype(BF)


def shift(array, axis, step):
    peers = lax.axis_size(axis)
    return lax.ppermute(array, axis, [(i, (i + step) % peers) for i in range(peers)])


def struct(shape, dtype):
    return jax.ShapeDtypeStruct(shape, dtype)


def on_device(disp, lift_w, conv1_w, reduce1_w, conv2_w, reduce2_w, conv3_w):
    own = disp.reshape(24, 8, 128)
    up = shift(own, "wide", 1)
    wl, w1, w2 = call(
        weights_kernel,
        (struct((8, 512, 256), BF), struct((12, 256, 256), BF), struct((12, 384, 256), BF)),
        (lift_w, conv1_w.reshape(9, 192, 64), conv2_w.reshape(9, 384, 128)),
        name="arrange_weights",
        flops=10**9,
        nbytes=7 * 10**6,
    )
    down = shift(own, "wide", -1)
    dt, left, right = call(
        turn_kernel,
        (struct((24, 144, 128), F32), struct((24, 8, 128), F32), struct((24, 8, 128), F32)),
        (up, own, down),
        name="columns_to_rows",
        flops=10**7,
        nbytes=2 * 10**6,
    )
    rrecv = shift(left, "narrow", -1)
    lrecv = shift(right, "narrow", 1)
    wr1 = reduce1_w.reshape(512, 128)
    fin, mid = call(
        inner_kernel,
        (struct((8, 8, 64, 128), BF), struct((4, 10, 64, 128), BF)),
        (dt, wl, w1, wr1),
        scratch=(
            VMEM((1536, 512), BF),
            VMEM((10, 24, 64, 256), BF),
            VMEM((8, 10, 2, 64, 128), BF),
        ),
        name="fine_inner",
        flops=8 * 10**9,
        nbytes=8 * 10**6,
    )
    hbm = pl.BlockSpec(memory_space=pl.ANY)
    whole = pl.BlockSpec(memory_space=VMEM)
    edge, skip, chunk = call(
        outer_kernel,
        (struct((8, 8, 16, 128), BF), struct((4, 4, 64, 128), BF), struct((64, 4, 128), F32)),
        (
            lrecv, left, right, rrecv, wl, w1, wr1, mid, w2,
            reduce2_w.reshape(1024, 256), conv3_w.reshape(3, 2304, 256),
        ),
        in_specs=[whole] * 8 + [hbm] * 3,
        scratch=(
            VMEM((24, 40, 128), F32),
            VMEM((384, 512), BF),
            VMEM((10, 24, 16, 256), BF),
            VMEM((8, 10, 2, 16, 128), BF),
            VMEM((4, 10, 16, 128), F32),
            VMEM((40, 88, 128), F32),
            VMEM((4, 10, 80, 384), BF),
            VMEM((4, 8, 80, 128), F32),
            VMEM((2, 4, 40, 256), F32),
            VMEM((12, 384, 256), BF),
            VMEM((1024, 256), BF),
            VMEM((3, 2304, 256), BF),
            pltpu.SemaphoreType.DMA((3,)),
        ),
        name="middle_and_coarse",
        flops=6 * 10**9,
        nbytes=12 * 10**6,
    )
    received = lax.all_to_all(chunk, "wide", 0, 0, tiled=True)
    finest = pl.pallas_call(
        finest_kernel,
        grid=(8,),
        out_shape=struct((64, 8, 8, 128), BF),
        in_specs=[
            pl.BlockSpec((1, 8, 64, 128), lambda p: (p, 0, 0, 0)),
            pl.BlockSpec((1, 8, 16, 128), lambda p: (p, 0, 0, 0)),
        ],
        out_specs=pl.BlockSpec((64, 1, 8, 128), lambda p: (0, p, 0, 0)),
        scratch_shapes=[VMEM((128, 128), F32), VMEM((64, 128), F32)],
        compiler_params=pltpu.CompilerParams(vmem_limit_bytes=LIMIT),
        cost_estimate=pl.CostEstimate(flops=10**8, bytes_accessed=3 * 10**6, transcendentals=0),
        name="finest_layout",
    )(fin, edge)
    coarse = call(
        coarse_kernel,
        struct((4, 2, 32, 128), BF),
        (received,),
        scratch=(VMEM((128, 128), F32),),
        name="coarse_layout",
        flops=10**6,
        nbytes=2 * 10**5,
    )
    return finest, skip.transpose(3, 0, 1, 2), coarse.transpose(0, 1, 3, 2)


def solution(mesh):
    return jax.shard_map(
        on_device,
        mesh=mesh,
        in_specs=(P(None, None, "wide", "narrow"), P(), P(), P(), P(), P(), P()),
        out_specs=(
            P(None, None, "wide", "narrow"),
            P(None, None, "wide", "narrow"),
            P("wide", None, None, "narrow"),
        ),
        check_vma=False,
    )
```

```python
import jax
import jax.numpy as jnp
from jax import lax
from jax.experimental import pallas as pl
from jax.experimental.pallas import tpu as pltpu
from jax.sharding import PartitionSpec as P

F32 = jnp.float32
BF = jnp.bfloat16
VMEM = pltpu.VMEM
MIB = 1024 * 1024


def leaky(v):
    return jnp.maximum(v, 0.01 * v)


def rounded(v):
    return v.astype(BF).astype(F32)


def mm(a, b):
    return jnp.dot(a, b, preferred_element_type=F32)


def call(kernel, outs, args, limit, scratch=(), name=None, flops=0, nbytes=0):
    whole = pl.BlockSpec(memory_space=VMEM)
    return pl.pallas_call(
        kernel,
        out_shape=outs,
        in_specs=[whole] * len(args),
        out_specs=jax.tree.map(lambda _: whole, outs),
        scratch_shapes=list(scratch),
        compiler_params=pltpu.CompilerParams(vmem_limit_bytes=limit * MIB),
        cost_estimate=pl.CostEstimate(flops=flops, bytes_accessed=nbytes, transcendentals=0),
        name=name,
    )(*args)


def fine_weights_kernel(lift_ref, c1_ref, wl_ref, w1_ref):
    w = lift_ref[...]
    hi = rounded(w)
    low = rounded(w - hi)
    place = (
        lax.broadcasted_iota(jnp.int32, (64, 256), 1) % 64
        == lax.broadcasted_iota(jnp.int32, (64, 256), 0)
    ).astype(BF)
    hi4 = mm(hi.astype(BF), place)
    low4 = mm(low.astype(BF), place)
    terms = []
    for s in range(5):
        for m in range(3):
            src = low4 if s in (1, 3) else hi4
            terms.append(jnp.broadcast_to(src[m : m + 1, :], (8, 256)))
    terms.append(jnp.zeros((8, 256), F32))
    base = jnp.concatenate(terms, axis=0)
    row = lax.broadcasted_iota(jnp.int32, (128, 256), 0) % 8
    lane = lax.broadcasted_iota(jnp.int32, (128, 256), 1)
    for t in range(4):
        for j in range(2):
            keep = (row == 2 * t + lane // 128) & (lane // 64 % 2 == j)
            wl_ref[t, j * 128 : (j + 1) * 128, :] = jnp.where(keep, base, 0.0).astype(BF)
    rows64 = lax.broadcasted_iota(jnp.int32, (64, 128), 0)
    lanes64 = lax.broadcasted_iota(jnp.int32, (64, 128), 1)
    left = (rows64 == lanes64).astype(BF)
    right = (rows64 + 64 == lanes64).astype(BF)
    zero1 = jnp.zeros((256, 128), BF)
    zero64 = jnp.zeros((64, 128), F32)
    for b in range(3):
        for a in range(3):
            k = c1_ref[a * 3 + b]
            pair = jnp.concatenate([mm(k, left), zero64], 0) + jnp.concatenate(
                [zero64, mm(k, right)], 0
            )
            pair = pair.astype(BF)
            w1_ref[a * 3 + b, :, 0:128] = pair
            w1_ref[(a + 1) * 3 + b, :, 128:256] = pair
        w1_ref[9 + b, :, 0:128] = zero1
        w1_ref[b, :, 128:256] = zero1


def middle_weights_kernel(c2_ref, w2_ref):
    zero2 = jnp.zeros((384, 128), BF)
    for b in range(3):
        for a in range(3):
            w2_ref[a * 3 + b, :, 0:128] = c2_ref[a * 3 + b]
            w2_ref[(a + 1) * 3 + b, :, 128:256] = c2_ref[a * 3 + b]
        w2_ref[9 + b, :, 0:128] = zero2
        w2_ref[b, :, 128:256] = zero2


def turn_kernel(up_ref, own_ref, down_ref, dt_ref, left_ref, right_ref):
    for plane in range(8):
        for blk, src in enumerate((up_ref, own_ref, down_ref)):
            parts = [[], [], []]
            for m in range(3):
                v = src[m * 8 + plane]
                hi = rounded(v)
                rest = v - hi
                mid = rounded(rest)
                parts[0].append(hi)
                parts[1].append(mid)
                parts[2].append(rest - mid)
            tiles = parts[0] + parts[0] + parts[1] + parts[1] + parts[2]
            tiles.append(jnp.zeros((8, 128), F32))
            turned = jnp.concatenate(tiles, axis=0).T
            g = plane * 3 + blk
            dt_ref[g, 8:136] = turned
            left_ref[g] = turned[0:8]
            right_ref[g] = turned[120:128]
    dt_ref[:, 0:8, :] = jnp.zeros((24, 8, 128), F32)
    dt_ref[:, 136:144, :] = jnp.zeros((24, 8, 128), F32)


def fine_levels(lhs_ref, wl_ref, w1_ref, wr1_ref, x4_ref, fn_ref, mid_ref, pairs, chunk):
    for t in range(4):
        for half in range(2):
            out = leaky(mm(lhs_ref[half], wl_ref[t])).astype(BF).astype(x4_ref.dtype)
            out = out.reshape(24, pairs, 256)
            lanes = slice(half * 128, (half + 1) * 128)
            for g in range(24):
                for r in range(2):
                    x4_ref[g // 3, (g % 3) * 8 + 2 * t + r, :, lanes] = out[
                        g, :, r * 128 : (r + 1) * 128
                    ]
    for pp in range(4):
        taps = [dp for dp in range(4) if 0 <= 2 * pp - 1 + dp < 8]
        weight = w1_ref[taps[0] * 3 : taps[-1] * 3 + 3].reshape(len(taps) * 768, 256)
        for r0 in range(0, 20, chunk):
            lhs = jnp.concatenate(
                [
                    x4_ref[2 * pp - 1 + dp, 1 + b + r0 : 1 + b + r0 + chunk].reshape(
                        chunk * pairs, 256
                    )
                    for dp in taps
                    for b in range(3)
                ],
                axis=1,
            ).astype(BF)
            out = leaky(mm(lhs, weight)).astype(BF).astype(fn_ref.dtype)
            for q in range(2):
                fn_ref[2 * pp + q, r0 // 2 : (r0 + chunk) // 2] = out[
                    :, q * 128 : (q + 1) * 128
                ].reshape(chunk // 2, 2, pairs, 128)
        lhs = jnp.concatenate(
            [
                fn_ref[2 * pp + a, :, b].reshape(10 * pairs, 128)
                for a in range(2)
                for b in range(2)
            ],
            axis=1,
        ).astype(BF)
        out = leaky(mm(lhs, wr1_ref[...])).astype(BF)
        mid_ref[pp] = out.astype(mid_ref.dtype).reshape(10, pairs, 128)


def inner_kernel(dt_ref, wl_ref, w1_ref, wr1_ref, fin_ref, mid_ref, lhs_ref, x4_ref, fn_ref):
    for g in range(24):
        for half in range(2):
            lhs_ref[half, g * 64 : (g + 1) * 64, :] = jnp.concatenate(
                [dt_ref[g, pl.ds(7 + 2 * half + j, 64, stride=2)] for j in range(2)], axis=1
            ).astype(BF)
    fine_levels(lhs_ref, wl_ref, w1_ref, wr1_ref, x4_ref, fn_ref, mid_ref, 64, 10)
    for plane in range(8):
        fin_ref[plane] = fn_ref[plane, 3:7].reshape(8, 64, 128)


def outer_kernel(
    lrecv_ref, left_ref, right_ref, rrecv_ref, wl_ref, w1_ref, wr1_ref, main_ref, w2_ref, wr2_ref, w3_ref,
    edge_ref, skip_ref, chunk_ref,
    de_ref, dw_ref, lhs_ref, x4_ref, fn_ref, me_ref, mf_ref, xm_ref, ms_ref, cf_ref,
):
    de_ref[:, 0:8] = lrecv_ref[...]
    de_ref[:, 8:16] = left_ref[...]
    de_ref[:, 16:24] = right_ref[...]
    de_ref[:, 24:32] = rrecv_ref[...]
    for half in range(2):
        dw_ref[half, :, 0:8] = de_ref[:, 1 + 2 * half : 9 + 2 * half]
        dw_ref[half, :, 8:16] = de_ref[:, 21 + 2 * half : 29 + 2 * half]
    for half in range(2):
        for g in range(0, 24, 2):
            lhs_ref[half, g * 8 : (g + 2) * 8, :] = jnp.concatenate(
                [
                    jnp.concatenate(
                        [dw_ref[half, g + k, pl.ds(j, 8, stride=2)] for k in range(2)], axis=0
                    )
                    for j in range(2)
                ],
                axis=1,
            ).astype(BF)
    fine_levels(lhs_ref, wl_ref, w1_ref, wr1_ref, x4_ref, fn_ref, me_ref, 8, 20)
    for plane in range(8):
        edge_ref[plane] = fn_ref[plane, 3:7].reshape(8, 8, 128)

    def merge(n, carry):
        plane, row = n // 10, n % 10
        mf_ref[n, 3:67] = main_ref[plane, row].astype(F32)
        mf_ref[n, 0:4] = me_ref[plane, row, 0:4]
        mf_ref[n, 66:70] = me_ref[plane, row, 4:8]
        for c in range(3):
            xm_ref[plane, row, :, c * 128 : (c + 1) * 128] = mf_ref[n, c : c + 80].astype(BF)
        return carry

    lax.fori_loop(0, 40, merge, 0)
    for half in range(2):
        taps = range(1, 4) if half == 0 else range(0, 3)
        lhs = jnp.concatenate(
            [
                xm_ref[2 * half - 1 + dp, b : b + 8].reshape(640, 384)
                for dp in taps
                for b in range(3)
            ],
            axis=1,
        )
        weight = w2_ref[taps[0] * 3 : taps[0] * 3 + 9].reshape(3456, 256)
        out = rounded(leaky(mm(lhs, weight)))
        for q in range(2):
            ms_ref[2 * half + q] = out[:, q * 128 : (q + 1) * 128].reshape(8, 80, 128)
    for plane in range(4):
        for row in range(4):
            skip_ref[plane, row] = ms_ref[plane, row + 2, 2:66].astype(BF)
    taps = []
    for a in range(2):
        for b in range(2):
            for c in range(2):
                taps.append(
                    jnp.concatenate(
                        [
                            ms_ref[2 * plane + a, 2 * row + b, pl.ds(c, 40, stride=2)]
                            for plane in range(2)
                            for row in range(4)
                        ],
                        axis=0,
                    )
                )
    lhs = jnp.concatenate(taps, axis=1).astype(BF)
    out = rounded(leaky(mm(lhs, wr2_ref[...])))
    cf_ref[...] = out.reshape(2, 4, 40, 256)
    lhs = []
    for plane in range(2):
        lhs.append(
            jnp.concatenate(
                [
                    jnp.concatenate(
                        [cf_ref[plane, row + b, c : c + 32] for row in range(2)], axis=0
                    )
                    for b in range(3)
                    for c in range(3)
                ],
                axis=1,
            ).astype(BF)
        )
    same = mm(jnp.concatenate(lhs, axis=0), w3_ref[1])
    first = same[0:64] + mm(lhs[1], w3_ref[2])
    second = same[64:128] + mm(lhs[0], w3_ref[0])
    out = jnp.concatenate([first[0:32], second[0:32], first[32:64], second[32:64]], axis=0)
    out = leaky(out).T
    chunk_ref[...] = out.reshape(64, 4, 128)


def finest_kernel(fin_ref, edge_ref, out_ref, wide_ref, rows_ref):
    lane = lax.broadcasted_iota(jnp.int32, (64, 128), 1)
    pair = lax.broadcasted_iota(jnp.int32, (64, 128), 0)
    for row in range(0, 8, 2):
        now = []
        for r in (row, row + 1):
            v = fin_ref[0, r].astype(F32)
            v = jnp.where(pair == 0, edge_ref[0, r, 3:4], v)
            now.append(jnp.where(pair == 63, edge_ref[0, r, 4:5], v))
        wide_ref[row // 2, pl.ds(0, 64, stride=2), :] = jnp.where(
            lane < 64, now[0], pltpu.roll(now[1], 64, 1)
        )
        wide_ref[row // 2, pl.ds(1, 64, stride=2), :] = jnp.where(
            lane < 64, pltpu.roll(now[0], 64, 1), now[1]
        )
        turned = wide_ref[row // 2].T
        rows_ref[:, row, :] = turned[0:64]
        rows_ref[:, row + 1, :] = turned[64:128]
    out_ref[:, 0] = rows_ref[...].astype(BF)


def coarse_kernel(in_ref, out_ref, y_ref):
    for c in range(4):
        v = in_ref[:, c, :]
        y_ref[pl.ds(0, 64, stride=2), :] = v
        y_ref[pl.ds(1, 64, stride=2), :] = pltpu.roll(v, 64, 1)
        out_ref[c] = y_ref[...].T[0:64].reshape(2, 32, 128).astype(BF)


def shift(array, axis, step):
    peers = lax.axis_size(axis)
    return lax.ppermute(array, axis, [(i, (i + step) % peers) for i in range(peers)])


def struct(shape, dtype):
    return jax.ShapeDtypeStruct(shape, dtype)


def on_device(disp, lift_w, conv1_w, reduce1_w, conv2_w, reduce2_w, conv3_w):
    own = disp.reshape(24, 8, 128)
    up = shift(own, "wide", 1)
    wl, w1 = call(
        fine_weights_kernel,
        (struct((4, 256, 256), BF), struct((12, 256, 256), BF)),
        (lift_w, conv1_w.reshape(9, 192, 64)),
        4,
        name="fine_weights",
        flops=10**9,
        nbytes=4 * 10**6,
    )
    again, wl = lax.optimization_barrier((own, wl))
    down = shift(again, "wide", -1)
    dt, left, right = call(
        turn_kernel,
        (struct((24, 144, 128), F32), struct((24, 8, 128), F32), struct((24, 8, 128), F32)),
        (up, own, down),
        6,
        name="columns_to_rows",
        flops=10**7,
        nbytes=2 * 10**6,
    )
    rrecv = shift(left, "narrow", -1)
    w2 = call(
        middle_weights_kernel,
        struct((12, 384, 256), BF),
        (conv2_w.reshape(9, 384, 128),),
        6,
        name="middle_weights",
        flops=10**6,
        nbytes=4 * 10**6,
    )
    again, w2 = lax.optimization_barrier((right, w2))
    lrecv = shift(again, "narrow", 1)
    wr1 = reduce1_w.reshape(512, 128)
    fin, mid = call(
        inner_kernel,
        (struct((8, 8, 64, 128), BF), struct((4, 10, 64, 128), BF)),
        (dt, wl, w1, wr1),
        24,
        scratch=(
            VMEM((2, 1536, 256), BF),
            VMEM((8, 24, 64, 256), BF),
            VMEM((8, 10, 2, 64, 128), BF),
        ),
        name="fine_inner",
        flops=8 * 10**9,
        nbytes=8 * 10**6,
    )
    edge, skip, chunk = call(
        outer_kernel,
        (struct((8, 8, 8, 128), F32), struct((4, 4, 64, 128), BF), struct((64, 4, 128), F32)),
        (
            lrecv, left, right, rrecv, wl, w1, wr1, mid, w2,
            reduce2_w.reshape(1024, 256), conv3_w.reshape(3, 2304, 256),
        ),
        32,
        scratch=(
            VMEM((24, 32, 128), F32),
            VMEM((2, 24, 16, 128), F32),
            VMEM((2, 192, 256), BF),
            VMEM((8, 24, 8, 256), F32),
            VMEM((8, 10, 2, 8, 128), F32),
            VMEM((4, 10, 8, 128), F32),
            VMEM((40, 88, 128), F32),
            VMEM((4, 10, 80, 384), BF),
            VMEM((4, 8, 80, 128), F32),
            VMEM((2, 4, 40, 256), F32),
        ),
        name="middle_and_coarse",
        flops=6 * 10**9,
        nbytes=12 * 10**6,
    )
    received = lax.all_to_all(chunk, "wide", 0, 0, tiled=True)
    finest = pl.pallas_call(
        finest_kernel,
        grid=(8,),
        out_shape=struct((64, 8, 8, 128), BF),
        in_specs=[
            pl.BlockSpec((1, 8, 64, 128), lambda p: (p, 0, 0, 0)),
            pl.BlockSpec((1, 8, 8, 128), lambda p: (p, 0, 0, 0)),
        ],
        out_specs=pl.BlockSpec((64, 1, 8, 128), lambda p: (0, p, 0, 0)),
        scratch_shapes=[VMEM((4, 128, 128), F32), VMEM((64, 8, 128), F32)],
        compiler_params=pltpu.CompilerParams(vmem_limit_bytes=6 * MIB),
        cost_estimate=pl.CostEstimate(flops=10**8, bytes_accessed=3 * 10**6, transcendentals=0),
        name="finest_layout",
    )(fin, edge)
    coarse = call(
        coarse_kernel,
        struct((4, 2, 32, 128), BF),
        (received,),
        4,
        scratch=(VMEM((128, 128), F32),),
        name="coarse_layout",
        flops=10**6,
        nbytes=2 * 10**5,
    )
    return finest, skip.transpose(3, 0, 1, 2), coarse.transpose(0, 1, 3, 2)


def solution(mesh):
    return jax.shard_map(
        on_device,
        mesh=mesh,
        in_specs=(P(None, None, "wide", "narrow"), P(), P(), P(), P(), P(), P()),
        out_specs=(
            P(None, None, "wide", "narrow"),
            P(None, None, "wide", "narrow"),
            P("wide", None, None, "narrow"),
        ),
        check_vma=False,
    )
```

```python
import jax
import jax.numpy as jnp
from jax import lax
from jax.experimental import pallas as pl
from jax.experimental.pallas import tpu as pltpu
from jax.sharding import PartitionSpec as P

F32 = jnp.float32
BF = jnp.bfloat16
VMEM = pltpu.VMEM
MIB = 1024 * 1024


def leaky(v):
    return jnp.maximum(v, 0.01 * v)


def rounded(v):
    return v.astype(BF).astype(F32)


def mm(a, b):
    return jnp.dot(a, b, preferred_element_type=F32)


def call(kernel, outs, args, limit, scratch=(), name=None, flops=0, nbytes=0, space=VMEM):
    whole = pl.BlockSpec(memory_space=VMEM)
    return pl.pallas_call(
        kernel,
        out_shape=outs,
        in_specs=[pl.BlockSpec(memory_space=space)] * len(args),
        out_specs=jax.tree.map(lambda _: whole, outs),
        scratch_shapes=list(scratch),
        compiler_params=pltpu.CompilerParams(vmem_limit_bytes=limit * MIB),
        cost_estimate=pl.CostEstimate(flops=flops, bytes_accessed=nbytes, transcendentals=0),
        name=name,
    )(*args)


def lift_weights(lift_ref, wl_ref):
    w = lift_ref[...]
    hi = rounded(w)
    low = rounded(w - hi)
    place = (
        lax.broadcasted_iota(jnp.int32, (64, 256), 1) % 64
        == lax.broadcasted_iota(jnp.int32, (64, 256), 0)
    ).astype(BF)
    hi4 = mm(hi.astype(BF), place)
    low4 = mm(low.astype(BF), place)
    terms = []
    for s in range(5):
        for m in range(3):
            src = low4 if s in (1, 3) else hi4
            terms.append(jnp.broadcast_to(src[m : m + 1, :], (8, 256)))
    terms.append(jnp.zeros((8, 256), F32))
    base = jnp.concatenate(terms, axis=0)
    row = lax.broadcasted_iota(jnp.int32, (128, 256), 0) % 8
    lane = lax.broadcasted_iota(jnp.int32, (128, 256), 1)
    for t in range(4):
        for j in range(2):
            keep = (row == 2 * t + lane // 128) & (lane // 64 % 2 == j)
            wl_ref[t, j * 128 : (j + 1) * 128, :] = jnp.where(keep, base, 0.0).astype(BF)


def conv1_weights(c1_ref, w1_ref):
    rows64 = lax.broadcasted_iota(jnp.int32, (64, 128), 0)
    lanes64 = lax.broadcasted_iota(jnp.int32, (64, 128), 1)
    left = (rows64 == lanes64).astype(BF)
    right = (rows64 + 64 == lanes64).astype(BF)
    zero1 = jnp.zeros((256, 128), BF)
    zero64 = jnp.zeros((64, 128), F32)
    for b in range(3):
        for a in range(3):
            k = c1_ref[a * 3 + b]
            pair = jnp.concatenate([mm(k, left), zero64], 0) + jnp.concatenate(
                [zero64, mm(k, right)], 0
            )
            pair = pair.astype(BF)
            w1_ref[a * 3 + b, :, 0:128] = pair
            w1_ref[(a + 1) * 3 + b, :, 128:256] = pair
        w1_ref[9 + b, :, 0:128] = zero1
        w1_ref[b, :, 128:256] = zero1


def middle_weights_kernel(c2_ref, w2_ref):
    zero2 = jnp.zeros((384, 128), BF)
    for b in range(3):
        for a in range(3):
            w2_ref[a * 3 + b, :, 0:128] = c2_ref[a * 3 + b]
            w2_ref[(a + 1) * 3 + b, :, 128:256] = c2_ref[a * 3 + b]
        w2_ref[9 + b, :, 0:128] = zero2
        w2_ref[b, :, 128:256] = zero2


def turned(src, plane):
    parts = [[], [], []]
    for m in range(3):
        v = src[m * 8 + plane]
        hi = rounded(v)
        rest = v - hi
        mid = rounded(rest)
        parts[0].append(hi)
        parts[1].append(mid)
        parts[2].append(rest - mid)
    tiles = parts[0] + parts[0] + parts[1] + parts[1] + parts[2]
    tiles.append(jnp.zeros((8, 128), F32))
    return jnp.concatenate(tiles, axis=0).T


def turn_block(src, dt_ref, left_ref, right_ref):
    for plane in range(8):
        out = turned(src, plane)
        dt_ref[plane, 8:136] = out
        left_ref[plane] = out[0:8]
        right_ref[plane] = out[120:128]
    dt_ref[:, 0:8, :] = jnp.zeros((8, 8, 128), F32)
    dt_ref[:, 136:144, :] = jnp.zeros((8, 8, 128), F32)


def turn_kernel(down_ref, lup_ref, rup_ref, lown_ref, rown_ref, dt_ref, left_ref, right_ref):
    turn_block(down_ref, dt_ref, left_ref.at[16:24], right_ref.at[16:24])
    left_ref[0:8] = lup_ref[...]
    right_ref[0:8] = rup_ref[...]
    left_ref[8:16] = lown_ref[...]
    right_ref[8:16] = rown_ref[...]


def window_columns(dt_ref, lhs_ref, groups):
    for g in range(groups):
        for half in range(2):
            lhs_ref[half, g * 64 : (g + 1) * 64, :] = jnp.concatenate(
                [dt_ref[g, pl.ds(7 + 2 * half + j, 64, stride=2)] for j in range(2)], axis=1
            ).astype(BF)


def lift(lhs_ref, wl_ref, groups, pairs, dtype, store):
    for t in range(4):
        for half in range(2):
            out = leaky(mm(lhs_ref[half], wl_ref[t])).astype(BF).astype(dtype)
            out = out.reshape(groups, pairs, 256)
            for g in range(groups):
                for r in range(2):
                    store(
                        g,
                        2 * t + r,
                        slice(half * 128, (half + 1) * 128),
                        out[g, :, r * 128 : (r + 1) * 128],
                    )


def conv1(lhs_of, w1_ref, pp):
    taps = [dp for dp in range(4) if 0 <= 2 * pp - 1 + dp < 8]
    weight = w1_ref[taps[0] * 3 : taps[-1] * 3 + 3].reshape(len(taps) * 768, 256)
    lhs = jnp.concatenate(
        [lhs_of(2 * pp - 1 + dp, b) for dp in taps for b in range(3)], axis=1
    ).astype(BF)
    return leaky(mm(lhs, weight)).astype(BF)


def reduce1(row_of, wr1_ref):
    lhs = jnp.concatenate(
        [
            jnp.concatenate([row_of(a, 2 * rr + b) for rr in range(10)], axis=0)
            for a in range(2)
            for b in range(2)
        ],
        axis=1,
    ).astype(BF)
    return leaky(mm(lhs, wr1_ref[...])).astype(BF)


def put_planes(out, pp, rows, fn_ref):
    for q in range(2):
        fn_ref[2 * pp + q] = out[:, q * 128 : (q + 1) * 128].reshape(rows, 64, 128)


def own_kernel(
    own_hbm, lift_hbm, c1_hbm, x4b_ref, fn_ref, lown_ref, rown_ref, wl_ref, w1_ref,
    dt_ref, lhs_ref, x4_ref, own_ref, lift_ref, c1_ref, sems,
):
    copies = [
        pltpu.make_async_copy(src, dst, sems.at[n])
        for n, (src, dst) in enumerate(
            ((own_hbm, own_ref), (lift_hbm, lift_ref), (c1_hbm, c1_ref))
        )
    ]
    for copy in copies:
        copy.start()
    copies[0].wait()
    turn_block(own_ref, dt_ref, lown_ref, rown_ref)
    copies[1].wait()
    lift_weights(lift_ref, wl_ref)
    copies[2].wait()
    conv1_weights(c1_ref, w1_ref)
    window_columns(dt_ref, lhs_ref, 8)

    def store(g, row, lanes, values):
        x4_ref[g, row, :, lanes] = values
        if row in (0, 1, 6, 7):
            x4b_ref[g, row if row < 2 else row - 4, :, lanes] = values

    lift(lhs_ref, wl_ref, 8, 64, BF, store)
    for pp in range(4):
        out = conv1(lambda plane, b: x4_ref[plane, b : b + 6].reshape(384, 256), w1_ref, pp)
        put_planes(out, pp, 6, fn_ref)


def top_kernel(up_ref, x4b_ref, wl_ref, w1_ref, fn_ref, lup_ref, rup_ref, dt_ref, lhs_ref, x4_ref):
    turn_block(up_ref, dt_ref, lup_ref, rup_ref)
    window_columns(dt_ref, lhs_ref, 8)

    def store(g, row, lanes, values):
        x4_ref[g, row, :, lanes] = values

    lift(lhs_ref, wl_ref, 8, 64, BF, store)
    for plane in range(8):
        x4_ref[plane, 8:10] = x4b_ref[plane, 0:2]
    for pp in range(4):
        out = conv1(
            lambda plane, b: x4_ref[plane, 1 + b : 8 + b].reshape(448, 256), w1_ref, pp
        )
        put_planes(out, pp, 7, fn_ref)


def bottom_kernel(
    dt_ref, x4b_ref, fnt_ref, fno_ref, wl_ref, w1_ref, wr1_ref, fn_ref, mid_ref, lhs_ref, x4_ref
):
    window_columns(dt_ref, lhs_ref, 8)

    def store(g, row, lanes, values):
        x4_ref[g, row + 2, :, lanes] = values

    lift(lhs_ref, wl_ref, 8, 64, BF, store)
    for plane in range(8):
        x4_ref[plane, 0:2] = x4b_ref[plane, 2:4]
    for pp in range(4):
        out = conv1(lambda plane, b: x4_ref[plane, b : b + 7].reshape(448, 256), w1_ref, pp)
        put_planes(out, pp, 7, fn_ref)
    for pp in range(4):

        def row_of(a, row):
            if row < 7:
                return fnt_ref[2 * pp + a, row]
            if row < 13:
                return fno_ref[2 * pp + a, row - 7]
            return fn_ref[2 * pp + a, row - 13]

        mid_ref[pp] = reduce1(row_of, wr1_ref).reshape(10, 64, 128)


def outer_kernel(
    lrecv_ref, left_ref, right_ref, rrecv_ref, wl_ref, w1_ref, wr1_ref, main_ref, w2_ref, wr2_ref, w3_ref,
    fn_ref, skip_ref, chunk_ref,
    de_ref, dw_ref, lhs_ref, x4_ref, me_ref, mf_ref, xm_ref, ms_ref, cf_ref,
):
    de_ref[:, 0:8] = lrecv_ref[...]
    de_ref[:, 8:16] = left_ref[...]
    de_ref[:, 16:24] = right_ref[...]
    de_ref[:, 24:32] = rrecv_ref[...]
    for half in range(2):
        dw_ref[half, :, 0:8] = de_ref[:, 1 + 2 * half : 9 + 2 * half]
        dw_ref[half, :, 8:16] = de_ref[:, 21 + 2 * half : 29 + 2 * half]
    for half in range(2):
        for g in range(0, 24, 2):
            lhs_ref[half, g * 8 : (g + 2) * 8, :] = jnp.concatenate(
                [
                    jnp.concatenate(
                        [dw_ref[half, g + k, pl.ds(j, 8, stride=2)] for k in range(2)], axis=0
                    )
                    for j in range(2)
                ],
                axis=1,
            ).astype(BF)

    def store(g, row, lanes, values):
        x4_ref[g % 8, g // 8 * 8 + row, :, lanes] = values

    lift(lhs_ref, wl_ref, 24, 8, F32, store)
    for pp in range(4):
        out = conv1(
            lambda plane, b: x4_ref[plane, 1 + b : 21 + b].reshape(160, 256), w1_ref, pp
        ).astype(F32)
        for q in range(2):
            fn_ref[2 * pp + q] = out[:, q * 128 : (q + 1) * 128].reshape(20, 8, 128)
        mid = reduce1(lambda a, row: fn_ref[2 * pp + a, row], wr1_ref)
        me_ref[pp] = mid.astype(F32).reshape(10, 8, 128)

    def merge(n, carry):
        plane, row = n // 10, n % 10
        mf_ref[n, 3:67] = main_ref[plane, row].astype(F32)
        mf_ref[n, 0:4] = me_ref[plane, row, 0:4]
        mf_ref[n, 66:70] = me_ref[plane, row, 4:8]
        for c in range(3):
            xm_ref[plane, row, :, c * 128 : (c + 1) * 128] = mf_ref[n, c : c + 80].astype(BF)
        return carry

    lax.fori_loop(0, 40, merge, 0)
    for half in range(2):
        taps = range(1, 4) if half == 0 else range(0, 3)
        lhs = jnp.concatenate(
            [
                xm_ref[2 * half - 1 + dp, b : b + 8].reshape(640, 384)
                for dp in taps
                for b in range(3)
            ],
            axis=1,
        )
        weight = w2_ref[taps[0] * 3 : taps[0] * 3 + 9].reshape(3456, 256)
        out = rounded(leaky(mm(lhs, weight)))
        for q in range(2):
            ms_ref[2 * half + q] = out[:, q * 128 : (q + 1) * 128].reshape(8, 80, 128)
    for plane in range(4):
        for row in range(4):
            skip_ref[plane, row] = ms_ref[plane, row + 2, 2:66].astype(BF)
    taps = []
    for a in range(2):
        for b in range(2):
            for c in range(2):
                taps.append(
                    jnp.concatenate(
                        [
                            ms_ref[2 * plane + a, 2 * row + b, pl.ds(c, 40, stride=2)]
                            for plane in range(2)
                            for row in range(4)
                        ],
                        axis=0,
                    )
                )
    lhs = jnp.concatenate(taps, axis=1).astype(BF)
    out = rounded(leaky(mm(lhs, wr2_ref[...])))
    cf_ref[...] = out.reshape(2, 4, 40, 256)
    lhs = []
    for plane in range(2):
        lhs.append(
            jnp.concatenate(
                [
                    jnp.concatenate(
                        [cf_ref[plane, row + b, c : c + 32] for row in range(2)], axis=0
                    )
                    for b in range(3)
                    for c in range(3)
                ],
                axis=1,
            ).astype(BF)
        )
    same = mm(jnp.concatenate(lhs, axis=0), w3_ref[1])
    first = same[0:64] + mm(lhs[1], w3_ref[2])
    second = same[64:128] + mm(lhs[0], w3_ref[0])
    out = jnp.concatenate([first[0:32], second[0:32], first[32:64], second[32:64]], axis=0)
    out = leaky(out).T
    chunk_ref[...] = out.reshape(64, 4, 128).astype(BF)


def finest_kernel(fnt_ref, fno_ref, fnb_ref, edge_ref, out_ref, wide_ref, rows_ref):
    lane = lax.broadcasted_iota(jnp.int32, (64, 128), 1)
    pair = lax.broadcasted_iota(jnp.int32, (64, 128), 0)
    for row in range(0, 8, 2):
        now = []
        for r in (row, row + 1):
            v = (fnt_ref[0, 0] if r == 0 else fnb_ref[0, 0] if r == 7 else fno_ref[0, r - 1]).astype(F32)
            v = jnp.where(pair == 0, edge_ref[0, r + 6, 3:4], v)
            now.append(jnp.where(pair == 63, edge_ref[0, r + 6, 4:5], v))
        wide_ref[row // 2, pl.ds(0, 64, stride=2), :] = jnp.where(
            lane < 64, now[0], pltpu.roll(now[1], 64, 1)
        )
        wide_ref[row // 2, pl.ds(1, 64, stride=2), :] = jnp.where(
            lane < 64, pltpu.roll(now[0], 64, 1), now[1]
        )
        turned = wide_ref[row // 2].T
        rows_ref[:, row, :] = turned[0:64]
        rows_ref[:, row + 1, :] = turned[64:128]
    out_ref[:, 0] = rows_ref[...].astype(BF)


def coarse_kernel(in_ref, out_ref, y_ref):
    all_in = in_ref[...].astype(F32)
    for c in range(4):
        v = all_in[:, c, :]
        y_ref[pl.ds(0, 64, stride=2), :] = v
        y_ref[pl.ds(1, 64, stride=2), :] = pltpu.roll(v, 64, 1)
        out_ref[c] = y_ref[...].T[0:64].reshape(2, 32, 128).astype(BF)


def shift(array, axis, step):
    peers = lax.axis_size(axis)
    return lax.ppermute(array, axis, [(i, (i + step) % peers) for i in range(peers)])


def struct(shape, dtype):
    return jax.ShapeDtypeStruct(shape, dtype)


def on_device(disp, lift_w, conv1_w, reduce1_w, conv2_w, reduce2_w, conv3_w):
    own = disp.reshape(24, 8, 128)
    up = shift(own, "wide", 1)
    strip = struct((8, 8, 128), F32)
    fine_scratch = (VMEM((2, 512, 256), BF), VMEM((8, 10, 64, 256), BF))
    turn_scratch = (VMEM((8, 144, 128), F32),)
    stay = lambda x: pltpu.with_memory_space_constraint(x, pltpu.HBM)
    x4b, fno, lown, rown, wl, w1 = call(
        own_kernel,
        (
            struct((8, 4, 64, 256), BF),
            struct((8, 6, 64, 128), BF),
            strip,
            strip,
            struct((4, 256, 256), BF),
            struct((12, 256, 256), BF),
        ),
        (stay(own), stay(lift_w), stay(conv1_w.reshape(9, 192, 64))),
        14,
        scratch=turn_scratch
        + fine_scratch
        + (
            VMEM((24, 8, 128), F32),
            VMEM((3, 64), F32),
            VMEM((9, 192, 64), BF),
            pltpu.SemaphoreType.DMA((3,)),
        ),
        name="fine_own_rows",
        flops=2 * 10**9,
        nbytes=6 * 10**6,
        space=pltpu.HBM,
    )
    again, x4b = lax.optimization_barrier((own, x4b))
    down = shift(again, "wide", -1)
    w2 = call(
        middle_weights_kernel,
        struct((12, 384, 256), BF),
        (conv2_w.reshape(9, 384, 128),),
        6,
        name="middle_weights",
        flops=10**6,
        nbytes=4 * 10**6,
    )
    fnt, lup, rup = call(
        top_kernel,
        (struct((8, 7, 64, 128), BF), strip, strip),
        (up, x4b, wl, w1),
        12,
        scratch=turn_scratch + fine_scratch,
        name="fine_top_rows",
        flops=3 * 10**9,
        nbytes=6 * 10**6,
    )
    dt, left, right = call(
        turn_kernel,
        (struct((8, 144, 128), F32), struct((24, 8, 128), F32), struct((24, 8, 128), F32)),
        (down, lup, rup, lown, rown),
        6,
        name="columns_to_rows",
        flops=10**7,
        nbytes=2 * 10**6,
    )
    rrecv = shift(left, "narrow", -1)
    lrecv = shift(right, "narrow", 1)
    wr1 = reduce1_w.reshape(512, 128)
    fnb, mid = call(
        bottom_kernel,
        (struct((8, 7, 64, 128), BF), struct((4, 10, 64, 128), BF)),
        (dt, x4b, fnt, fno, wl, w1, wr1),
        14,
        scratch=fine_scratch,
        name="fine_bottom_rows",
        flops=8 * 10**9,
        nbytes=6 * 10**6,
    )
    edge, skip, chunk = call(
        outer_kernel,
        (struct((8, 20, 8, 128), F32), struct((4, 4, 64, 128), BF), struct((64, 4, 128), BF)),
        (
            lrecv, left, right, rrecv, wl, w1, wr1, mid, w2,
            reduce2_w.reshape(1024, 256), conv3_w.reshape(3, 2304, 256),
        ),
        24,
        scratch=(
            VMEM((24, 32, 128), F32),
            VMEM((2, 24, 16, 128), F32),
            VMEM((2, 192, 256), BF),
            VMEM((8, 24, 8, 256), F32),
            VMEM((4, 10, 8, 128), F32),
            VMEM((40, 88, 128), F32),
            VMEM((4, 10, 80, 384), BF),
            VMEM((4, 8, 80, 128), F32),
            VMEM((2, 4, 40, 256), F32),
        ),
        name="middle_and_coarse",
        flops=6 * 10**9,
        nbytes=12 * 10**6,
    )
    received = lax.all_to_all(chunk, "wide", 0, 0, tiled=True)
    finest = pl.pallas_call(
        finest_kernel,
        grid=(8,),
        out_shape=struct((64, 8, 8, 128), BF),
        in_specs=[
            pl.BlockSpec((1, 1, 64, 128), lambda p: (p, 6, 0, 0)),
            pl.BlockSpec((1, 6, 64, 128), lambda p: (p, 0, 0, 0)),
            pl.BlockSpec((1, 1, 64, 128), lambda p: (p, 0, 0, 0)),
            pl.BlockSpec((1, 20, 8, 128), lambda p: (p, 0, 0, 0)),
        ],
        out_specs=pl.BlockSpec((64, 1, 8, 128), lambda p: (0, p, 0, 0)),
        scratch_shapes=[VMEM((4, 128, 128), F32), VMEM((64, 8, 128), F32)],
        compiler_params=pltpu.CompilerParams(vmem_limit_bytes=6 * MIB),
        cost_estimate=pl.CostEstimate(flops=10**8, bytes_accessed=3 * 10**6, transcendentals=0),
        name="finest_layout",
    )(fnt, fno, fnb, edge)
    coarse = call(
        coarse_kernel,
        struct((4, 2, 32, 128), BF),
        (received,),
        4,
        scratch=(VMEM((128, 128), F32),),
        name="coarse_layout",
        flops=10**6,
        nbytes=2 * 10**5,
    )
    return finest, skip.transpose(3, 0, 1, 2), coarse.transpose(0, 1, 3, 2)


def solution(mesh):
    return jax.shard_map(
        on_device,
        mesh=mesh,
        in_specs=(P(None, None, "wide", "narrow"), P(), P(), P(), P(), P(), P()),
        out_specs=(
            P(None, None, "wide", "narrow"),
            P(None, None, "wide", "narrow"),
            P("wide", None, None, "narrow"),
        ),
        check_vma=False,
    )
```

```python
import jax
import jax.numpy as jnp
from jax import lax
from jax.experimental import pallas as pl
from jax.experimental.pallas import tpu as pltpu
from jax.sharding import PartitionSpec as P

F32 = jnp.float32
BF = jnp.bfloat16
VMEM = pltpu.VMEM
MIB = 1024 * 1024


def leaky(v):
    return jnp.maximum(v, 0.01 * v)


def rounded(v):
    return v.astype(BF).astype(F32)


def mm(a, b):
    return jnp.dot(a, b, preferred_element_type=F32)


def call(kernel, outs, args, limit, scratch=(), name=None, flops=0, nbytes=0, space=VMEM, last=None):
    whole = pl.BlockSpec(memory_space=VMEM)
    return pl.pallas_call(
        kernel,
        out_shape=outs,
        in_specs=[pl.BlockSpec(memory_space=space)] * (len(args) - 1)
        + [pl.BlockSpec(memory_space=last or space)],
        out_specs=jax.tree.map(lambda _: whole, outs),
        scratch_shapes=list(scratch),
        compiler_params=pltpu.CompilerParams(vmem_limit_bytes=limit * MIB),
        cost_estimate=pl.CostEstimate(flops=flops, bytes_accessed=nbytes, transcendentals=0),
        name=name,
    )(*args)


def lift_weights(lift_ref, wl_ref):
    w = lift_ref[...]
    hi = rounded(w)
    low = rounded(w - hi)
    place = (
        lax.broadcasted_iota(jnp.int32, (64, 256), 1) % 64
        == lax.broadcasted_iota(jnp.int32, (64, 256), 0)
    ).astype(BF)
    hi4 = mm(hi.astype(BF), place)
    low4 = mm(low.astype(BF), place)
    terms = []
    for s in range(5):
        for m in range(3):
            src = low4 if s in (1, 3) else hi4
            terms.append(jnp.broadcast_to(src[m : m + 1, :], (8, 256)))
    terms.append(jnp.zeros((8, 256), F32))
    base = jnp.concatenate(terms, axis=0)
    row = lax.broadcasted_iota(jnp.int32, (128, 256), 0) % 8
    lane = lax.broadcasted_iota(jnp.int32, (128, 256), 1)
    for t in range(4):
        for j in range(2):
            keep = (row == 2 * t + lane // 128) & (lane // 64 % 2 == j)
            wl_ref[t, j * 128 : (j + 1) * 128, :] = jnp.where(keep, base, 0.0).astype(BF)


def conv1_weights(c1_ref, w1_ref):
    rows64 = lax.broadcasted_iota(jnp.int32, (64, 128), 0)
    lanes64 = lax.broadcasted_iota(jnp.int32, (64, 128), 1)
    left = (rows64 == lanes64).astype(BF)
    right = (rows64 + 64 == lanes64).astype(BF)
    zero1 = jnp.zeros((256, 128), BF)
    zero64 = jnp.zeros((64, 128), F32)
    for b in range(3):
        for a in range(3):
            k = c1_ref[a * 3 + b]
            pair = jnp.concatenate([mm(k, left), zero64], 0) + jnp.concatenate(
                [zero64, mm(k, right)], 0
            )
            pair = pair.astype(BF)
            w1_ref[a * 3 + b, :, 0:128] = pair
            w1_ref[(a + 1) * 3 + b, :, 128:256] = pair
        w1_ref[9 + b, :, 0:128] = zero1
        w1_ref[b, :, 128:256] = zero1


def turned(src, plane):
    parts = [[], [], []]
    for m in range(3):
        v = src[m * 8 + plane]
        hi = rounded(v)
        rest = v - hi
        mid = rounded(rest)
        parts[0].append(hi)
        parts[1].append(mid)
        parts[2].append(rest - mid)
    tiles = parts[0] + parts[0] + parts[1] + parts[1] + parts[2]
    tiles.append(jnp.zeros((8, 128), F32))
    return jnp.concatenate(tiles, axis=0).T


def turn_block(src, dt_ref, left_ref, right_ref):
    for plane in range(8):
        out = turned(src, plane)
        dt_ref[plane, 8:136] = out
        left_ref[plane] = out[0:8]
        right_ref[plane] = out[120:128]
    dt_ref[:, 0:8, :] = jnp.zeros((8, 8, 128), F32)
    dt_ref[:, 136:144, :] = jnp.zeros((8, 8, 128), F32)


def turn_kernel(down_ref, lup_ref, rup_ref, lown_ref, rown_ref, dt_ref, left_ref, right_ref):
    turn_block(down_ref, dt_ref, left_ref.at[16:24], right_ref.at[16:24])
    left_ref[0:8] = lup_ref[...]
    right_ref[0:8] = rup_ref[...]
    left_ref[8:16] = lown_ref[...]
    right_ref[8:16] = rown_ref[...]


def window_columns(dt_ref, lhs_ref, groups):
    for g in range(groups):
        for half in range(2):
            lhs_ref[half, g * 64 : (g + 1) * 64, :] = jnp.concatenate(
                [dt_ref[g, pl.ds(7 + 2 * half + j, 64, stride=2)] for j in range(2)], axis=1
            ).astype(BF)


def lift(lhs_ref, wl_ref, groups, pairs, dtype, store):
    for t in range(4):
        for half in range(2):
            out = leaky(mm(lhs_ref[half], wl_ref[t])).astype(BF).astype(dtype)
            out = out.reshape(groups, pairs, 256)
            for g in range(groups):
                for r in range(2):
                    store(
                        g,
                        2 * t + r,
                        slice(half * 128, (half + 1) * 128),
                        out[g, :, r * 128 : (r + 1) * 128],
                    )


PAIRS = (
    (0, 1, (1, 2, 3)),
    (1, 1, (0, 1, 2, 3)),
    (2, 1, (0, 1, 2, 3)),
    (3, 1, (0, 1, 2)),
)


def conv1(lhs_of, w1_ref, taps):
    weight = w1_ref[taps[0] * 3 : taps[-1] * 3 + 3].reshape(len(taps) * 768, 256)
    lhs = jnp.concatenate(
        [lhs_of((dp - 1) // 2, (dp + 1) % 2, b) for dp in taps for b in range(3)], axis=1
    ).astype(BF)
    return leaky(mm(lhs, weight)).astype(BF)


def conv1_rows(x4_ref, w1_ref, fn_ref, first, rows):
    for pp, n, taps in PAIRS:
        out = conv1(
            lambda h, s, b: x4_ref[
                pp + h : pp + h + n, s, first + b : first + b + rows
            ].reshape(n * rows * 64, 256),
            w1_ref,
            taps,
        )
        for q in range(2):
            fn_ref[pp : pp + n, q] = out[:, q * 128 : (q + 1) * 128].reshape(n, rows, 64, 128)


def reduce1(taps, wr1_ref):
    lhs = jnp.concatenate(taps, axis=1).astype(BF)
    return leaky(mm(lhs, wr1_ref[...])).astype(BF)


def own_kernel(
    own_hbm, lift_hbm, c1_hbm, x4b_ref, fn_ref, lown_ref, rown_ref, wl_ref, w1_ref,
    dt_ref, lhs_ref, x4_ref, own_ref, lift_ref, c1_ref, sems,
):
    copies = [
        pltpu.make_async_copy(src, dst, sems.at[n])
        for n, (src, dst) in enumerate(
            ((own_hbm, own_ref), (lift_hbm, lift_ref), (c1_hbm, c1_ref))
        )
    ]
    for copy in copies:
        copy.start()
    copies[0].wait()
    turn_block(own_ref, dt_ref, lown_ref, rown_ref)
    copies[1].wait()
    lift_weights(lift_ref, wl_ref)
    copies[2].wait()
    conv1_weights(c1_ref, w1_ref)
    window_columns(dt_ref, lhs_ref, 8)

    def store(g, row, lanes, values):
        x4_ref[g // 2, g % 2, row, :, lanes] = values
        if row in (0, 1, 6, 7):
            x4b_ref[g, row if row < 2 else row - 4, :, lanes] = values

    lift(lhs_ref, wl_ref, 8, 64, BF, store)
    conv1_rows(x4_ref, w1_ref, fn_ref, 0, 6)


def top_kernel(up_ref, x4b_ref, wl_ref, w1_ref, fn_ref, lup_ref, rup_ref, dt_ref, lhs_ref, x4_ref):
    turn_block(up_ref, dt_ref, lup_ref, rup_ref)
    window_columns(dt_ref, lhs_ref, 8)

    def store(g, row, lanes, values):
        x4_ref[g // 2, g % 2, row, :, lanes] = values

    lift(lhs_ref, wl_ref, 8, 64, BF, store)
    for plane in range(8):
        x4_ref[plane // 2, plane % 2, 8:10] = x4b_ref[plane, 0:2]
    conv1_rows(x4_ref, w1_ref, fn_ref, 1, 7)


def bottom_kernel(
    dt_ref, x4b_ref, fnt_ref, fno_ref, wl_ref, w1_ref, wr1_ref, fn_ref, mid_ref, lhs_ref, x4_ref
):
    window_columns(dt_ref, lhs_ref, 8)

    def store(g, row, lanes, values):
        x4_ref[g // 2, g % 2, row + 2, :, lanes] = values

    lift(lhs_ref, wl_ref, 8, 64, BF, store)
    for plane in range(8):
        x4_ref[plane // 2, plane % 2, 0:2] = x4b_ref[plane, 2:4]
    conv1_rows(x4_ref, w1_ref, fn_ref, 0, 7)
    for pp in range(4):

        def row_of(a, row):
            if row < 7:
                return fnt_ref[pp, a, row]
            if row < 13:
                return fno_ref[pp, a, row - 7]
            return fn_ref[pp, a, row - 13]

        taps = [
            jnp.concatenate([row_of(a, 2 * rr + b) for rr in range(10)], axis=0)
            for a in range(2)
            for b in range(2)
        ]
        mid_ref[pp] = reduce1(taps, wr1_ref).reshape(10, 64, 128)


def outer_kernel(
    lrecv_ref, left_ref, right_ref, rrecv_ref, wl_ref, w1_ref, wr1_ref, main_ref, wr2_ref, w3_ref, c2_hbm,
    edge_ref, skip_ref, chunk_ref,
    de_ref, dw_ref, lhs_ref, x4_ref, fn_ref, me_ref, mf_ref, xm_ref, ms_ref, cf_ref, w2_ref, sem,
):
    copies = [
        pltpu.make_async_copy(
            c2_hbm, w2_ref.at[3 * q : 3 * q + 9, :, q * 128 : (q + 1) * 128], sem.at[q]
        )
        for q in range(2)
    ]
    for copy in copies:
        copy.start()
    w2_ref[0:3, :, 128:256] = jnp.zeros((3, 384, 128), BF)
    w2_ref[9:12, :, 0:128] = jnp.zeros((3, 384, 128), BF)
    de_ref[:, 0:8] = lrecv_ref[...]
    de_ref[:, 8:16] = left_ref[...]
    de_ref[:, 16:24] = right_ref[...]
    de_ref[:, 24:32] = rrecv_ref[...]
    for half in range(2):
        dw_ref[half, :, 0:8] = de_ref[:, 1 + 2 * half : 9 + 2 * half]
        dw_ref[half, :, 8:16] = de_ref[:, 21 + 2 * half : 29 + 2 * half]
    for half in range(2):
        for g in range(0, 24, 2):
            lhs_ref[half, g * 8 : (g + 2) * 8, :] = jnp.concatenate(
                [
                    jnp.concatenate(
                        [dw_ref[half, g + k, pl.ds(j, 8, stride=2)] for k in range(2)], axis=0
                    )
                    for j in range(2)
                ],
                axis=1,
            ).astype(BF)

    zero = jnp.zeros((24, 8, 256), F32)
    x4_ref[0, 1] = zero
    x4_ref[5, 0] = zero

    def store(g, row, lanes, values):
        x4_ref[1 + g % 8 // 2, g % 2, g // 8 * 8 + row, :, lanes] = values

    lift(lhs_ref, wl_ref, 24, 8, F32, store)
    out = conv1(
        lambda h, s, b: x4_ref[1 + h : 5 + h, s, 1 + b : 21 + b].reshape(640, 256),
        w1_ref,
        range(4),
    ).astype(F32)
    for q in range(2):
        fn_ref[:, q] = out[:, q * 128 : (q + 1) * 128].reshape(4, 10, 2, 8, 128)
    edge_ref[...] = fn_ref[:, :, 3:7].reshape(8, 8, 8, 128)
    taps = [fn_ref[:, a, :, b].reshape(320, 128) for a in range(2) for b in range(2)]
    me_ref[...] = reduce1(taps, wr1_ref).astype(F32).reshape(4, 10, 8, 128)

    def merge(n, carry):
        plane, row = n // 10, n % 10
        mf_ref[n, 16:80] = main_ref[plane, row].astype(F32)
        mf_ref[n, 13:17] = me_ref[plane, row, 0:4]
        mf_ref[n, 79:83] = me_ref[plane, row, 4:8]
        for c in range(3):
            xm_ref[plane, row, :, c * 128 : (c + 1) * 128] = mf_ref[n, 7 + c : 87 + c].astype(BF)
        return carry

    lax.fori_loop(0, 40, merge, 0)
    for copy in copies:
        copy.wait()
    for half in range(2):
        taps = range(1, 4) if half == 0 else range(0, 3)
        lhs = jnp.concatenate(
            [
                xm_ref[2 * half - 1 + dp, b : b + 8].reshape(640, 384)
                for dp in taps
                for b in range(3)
            ],
            axis=1,
        )
        weight = w2_ref[taps[0] * 3 : taps[0] * 3 + 9].reshape(3456, 256)
        out = rounded(leaky(mm(lhs, weight)))
        for q in range(2):
            ms_ref[2 * half + q, :, 0:80] = out[:, q * 128 : (q + 1) * 128].reshape(8, 80, 128)
    for plane in range(4):
        skip_ref[plane] = ms_ref[plane, 2:6, 8:72].astype(BF)
    taps = []
    for a in range(2):
        for b in range(2):
            for c in range(2):
                taps.append(
                    jnp.concatenate(
                        [
                            ms_ref[2 * plane + a, 2 * row + b, pl.ds(6 + c, 40, stride=2)]
                            for plane in range(2)
                            for row in range(4)
                        ],
                        axis=0,
                    )
                )
    lhs = jnp.concatenate(taps, axis=1).astype(BF)
    out = rounded(leaky(mm(lhs, wr2_ref[...])))
    cf_ref[...] = out.reshape(2, 4, 40, 256)
    lhs = []
    for plane in range(2):
        lhs.append(
            jnp.concatenate(
                [
                    jnp.concatenate(
                        [cf_ref[plane, row + b, c : c + 32] for row in range(2)], axis=0
                    )
                    for b in range(3)
                    for c in range(3)
                ],
                axis=1,
            ).astype(BF)
        )
    same = mm(jnp.concatenate(lhs, axis=0), w3_ref[1])
    first = same[0:64] + mm(lhs[1], w3_ref[2])
    second = same[64:128] + mm(lhs[0], w3_ref[0])
    out = jnp.concatenate([first[0:32], second[0:32], first[32:64], second[32:64]], axis=0)
    out = leaky(out).T
    chunk_ref[...] = out.reshape(64, 4, 128).astype(BF)


def finest_kernel(fnt_ref, fno_ref, fnb_ref, edge_ref, out_ref, wide_ref, rows_ref):
    lane = lax.broadcasted_iota(jnp.int32, (64, 128), 1)
    pair = lax.broadcasted_iota(jnp.int32, (64, 128), 0)
    for row in range(0, 8, 2):
        now = []
        for r in (row, row + 1):
            v = (fnt_ref[0, 0] if r == 0 else fnb_ref[0, 0] if r == 7 else fno_ref[0, r - 1]).astype(F32)
            v = jnp.where(pair == 0, edge_ref[0, r, 3:4], v)
            now.append(jnp.where(pair == 63, edge_ref[0, r, 4:5], v))
        wide_ref[row // 2, pl.ds(0, 64, stride=2), :] = jnp.where(
            lane < 64, now[0], pltpu.roll(now[1], 64, 1)
        )
        wide_ref[row // 2, pl.ds(1, 64, stride=2), :] = jnp.where(
            lane < 64, pltpu.roll(now[0], 64, 1), now[1]
        )
        turned = wide_ref[row // 2].T
        rows_ref[:, row, :] = turned[0:64]
        rows_ref[:, row + 1, :] = turned[64:128]
    out_ref[:, 0] = rows_ref[...].astype(BF)


def coarse_kernel(in_ref, out_ref, y_ref):
    all_in = in_ref[...].astype(F32)
    for c in range(4):
        v = all_in[:, c, :]
        y_ref[pl.ds(0, 64, stride=2), :] = v
        y_ref[pl.ds(1, 64, stride=2), :] = pltpu.roll(v, 64, 1)
        out_ref[c] = y_ref[...].T[0:64].reshape(2, 32, 128).astype(BF)


def shift(array, axis, step):
    peers = lax.axis_size(axis)
    return lax.ppermute(array, axis, [(i, (i + step) % peers) for i in range(peers)])


def struct(shape, dtype):
    return jax.ShapeDtypeStruct(shape, dtype)


def on_device(disp, lift_w, conv1_w, reduce1_w, conv2_w, reduce2_w, conv3_w):
    own = disp.reshape(24, 8, 128)
    up = shift(own, "wide", 1)
    strip = struct((8, 8, 128), F32)
    fine_scratch = (VMEM((2, 512, 256), BF), VMEM((4, 2, 10, 64, 256), BF))
    turn_scratch = (VMEM((8, 144, 128), F32),)
    stay = lambda x: pltpu.with_memory_space_constraint(x, pltpu.HBM)
    x4b, fno, lown, rown, wl, w1 = call(
        own_kernel,
        (
            struct((8, 4, 64, 256), BF),
            struct((4, 2, 6, 64, 128), BF),
            strip,
            strip,
            struct((4, 256, 256), BF),
            struct((12, 256, 256), BF),
        ),
        (stay(own), stay(lift_w), stay(conv1_w.reshape(9, 192, 64))),
        14,
        scratch=turn_scratch
        + fine_scratch
        + (
            VMEM((24, 8, 128), F32),
            VMEM((3, 64), F32),
            VMEM((9, 192, 64), BF),
            pltpu.SemaphoreType.DMA((3,)),
        ),
        name="fine_own_rows",
        flops=2 * 10**9,
        nbytes=6 * 10**6,
        space=pltpu.HBM,
    )
    again, x4b = lax.optimization_barrier((own, x4b))
    down = shift(again, "wide", -1)
    fnt, lup, rup = call(
        top_kernel,
        (struct((4, 2, 7, 64, 128), BF), strip, strip),
        (up, x4b, wl, w1),
        12,
        scratch=turn_scratch + fine_scratch,
        name="fine_top_rows",
        flops=3 * 10**9,
        nbytes=6 * 10**6,
    )
    dt, left, right = call(
        turn_kernel,
        (struct((8, 144, 128), F32), struct((24, 8, 128), F32), struct((24, 8, 128), F32)),
        (down, lup, rup, lown, rown),
        6,
        name="columns_to_rows",
        flops=10**7,
        nbytes=2 * 10**6,
    )
    rrecv = shift(left, "narrow", -1)
    lrecv = shift(right, "narrow", 1)
    wr1 = reduce1_w.reshape(512, 128)
    fnb, mid = call(
        bottom_kernel,
        (struct((4, 2, 7, 64, 128), BF), struct((4, 10, 64, 128), BF)),
        (dt, x4b, fnt, fno, wl, w1, wr1),
        14,
        scratch=fine_scratch,
        name="fine_bottom_rows",
        flops=8 * 10**9,
        nbytes=6 * 10**6,
    )
    edge, skip, chunk = call(
        outer_kernel,
        (struct((8, 8, 8, 128), F32), struct((4, 4, 64, 128), BF), struct((64, 4, 128), BF)),
        (
            lrecv, left, right, rrecv, wl, w1, wr1, mid,
            reduce2_w.reshape(1024, 256), conv3_w.reshape(3, 2304, 256),
            stay(conv2_w.reshape(9, 384, 128)),
        ),
        26,
        last=pltpu.HBM,
        scratch=(
            VMEM((24, 32, 128), F32),
            VMEM((2, 24, 16, 128), F32),
            VMEM((2, 192, 256), BF),
            VMEM((6, 2, 24, 8, 256), F32),
            VMEM((4, 2, 10, 2, 8, 128), F32),
            VMEM((4, 10, 8, 128), F32),
            VMEM((40, 96, 128), F32),
            VMEM((4, 10, 80, 384), BF),
            VMEM((4, 8, 88, 128), F32),
            VMEM((2, 4, 40, 256), F32),
            VMEM((12, 384, 256), BF),
            pltpu.SemaphoreType.DMA((2,)),
        ),
        name="middle_and_coarse",
        flops=6 * 10**9,
        nbytes=12 * 10**6,
    )
    received = lax.all_to_all(chunk, "wide", 0, 0, tiled=True)
    finest = pl.pallas_call(
        finest_kernel,
        grid=(8,),
        out_shape=struct((64, 8, 8, 128), BF),
        in_specs=[
            pl.BlockSpec((1, 1, 64, 128), lambda p: (p, 6, 0, 0)),
            pl.BlockSpec((1, 6, 64, 128), lambda p: (p, 0, 0, 0)),
            pl.BlockSpec((1, 1, 64, 128), lambda p: (p, 0, 0, 0)),
            pl.BlockSpec((1, 8, 8, 128), lambda p: (p, 0, 0, 0)),
        ],
        out_specs=pl.BlockSpec((64, 1, 8, 128), lambda p: (0, p, 0, 0)),
        scratch_shapes=[VMEM((4, 128, 128), F32), VMEM((64, 8, 128), F32)],
        compiler_params=pltpu.CompilerParams(vmem_limit_bytes=6 * MIB),
        cost_estimate=pl.CostEstimate(flops=10**8, bytes_accessed=3 * 10**6, transcendentals=0),
        name="finest_layout",
    )(
        fnt.reshape(8, 7, 64, 128),
        fno.reshape(8, 6, 64, 128),
        fnb.reshape(8, 7, 64, 128),
        edge,
    )
    coarse = call(
        coarse_kernel,
        struct((4, 2, 32, 128), BF),
        (received,),
        4,
        scratch=(VMEM((128, 128), F32),),
        name="coarse_layout",
        flops=10**6,
        nbytes=2 * 10**5,
    )
    return finest, skip.transpose(3, 0, 1, 2), coarse.transpose(0, 1, 3, 2)


def solution(mesh):
    return jax.shard_map(
        on_device,
        mesh=mesh,
        in_specs=(P(None, None, "wide", "narrow"), P(), P(), P(), P(), P(), P()),
        out_specs=(
            P(None, None, "wide", "narrow"),
            P(None, None, "wide", "narrow"),
            P("wide", None, None, "narrow"),
        ),
        check_vma=False,
    )
```

```python
import jax
import jax.numpy as jnp
from jax import lax
from jax.experimental import pallas as pl
from jax.experimental.pallas import tpu as pltpu
from jax.sharding import PartitionSpec as P

F32 = jnp.float32
BF = jnp.bfloat16
VMEM = pltpu.VMEM
MIB = 1024 * 1024


def leaky(v):
    return jnp.maximum(v, 0.01 * v)


def rounded(v):
    return v.astype(BF).astype(F32)


def mm(a, b):
    return jnp.dot(a, b, preferred_element_type=F32)


def call(kernel, outs, args, limit, scratch=(), name=None, flops=0, nbytes=0, space=VMEM, last=None):
    whole = pl.BlockSpec(memory_space=VMEM)
    return pl.pallas_call(
        kernel,
        out_shape=outs,
        in_specs=[pl.BlockSpec(memory_space=space)] * (len(args) - 1)
        + [pl.BlockSpec(memory_space=last or space)],
        out_specs=jax.tree.map(lambda _: whole, outs),
        scratch_shapes=list(scratch),
        compiler_params=pltpu.CompilerParams(vmem_limit_bytes=limit * MIB),
        cost_estimate=pl.CostEstimate(flops=flops, bytes_accessed=nbytes, transcendentals=0),
        name=name,
    )(*args)


def lift_weights(lift_ref, wl_ref):
    w = lift_ref[...]
    hi = rounded(w)
    low = rounded(w - hi)
    place = (
        lax.broadcasted_iota(jnp.int32, (64, 256), 1) % 64
        == lax.broadcasted_iota(jnp.int32, (64, 256), 0)
    ).astype(BF)
    hi4 = mm(hi.astype(BF), place)
    low4 = mm(low.astype(BF), place)
    terms = []
    for s in range(5):
        for m in range(3):
            src = low4 if s in (1, 3) else hi4
            terms.append(jnp.broadcast_to(src[m : m + 1, :], (8, 256)))
    terms.append(jnp.zeros((8, 256), F32))
    base = jnp.concatenate(terms, axis=0)
    row = lax.broadcasted_iota(jnp.int32, (128, 256), 0) % 8
    lane = lax.broadcasted_iota(jnp.int32, (128, 256), 1)
    for t in range(4):
        for j in range(2):
            keep = (row == 2 * t + lane // 128) & (lane // 64 % 2 == j)
            wl_ref[t, j * 128 : (j + 1) * 128, :] = jnp.where(keep, base, 0.0).astype(BF)


def conv1_weights(c1_ref, w1_ref):
    rows64 = lax.broadcasted_iota(jnp.int32, (64, 128), 0)
    lanes64 = lax.broadcasted_iota(jnp.int32, (64, 128), 1)
    left = (rows64 == lanes64).astype(BF)
    right = (rows64 + 64 == lanes64).astype(BF)
    zero1 = jnp.zeros((256, 128), BF)
    zero64 = jnp.zeros((64, 128), F32)
    for b in range(3):
        for a in range(3):
            k = c1_ref[a * 3 + b]
            pair = jnp.concatenate([mm(k, left), zero64], 0) + jnp.concatenate(
                [zero64, mm(k, right)], 0
            )
            pair = pair.astype(BF)
            w1_ref[a * 3 + b, :, 0:128] = pair
            w1_ref[(a + 1) * 3 + b, :, 128:256] = pair
        w1_ref[9 + b, :, 0:128] = zero1
        w1_ref[b, :, 128:256] = zero1


def turned(src, plane):
    parts = [[], [], []]
    for m in range(3):
        v = src[m * 8 + plane]
        hi = rounded(v)
        rest = v - hi
        mid = rounded(rest)
        parts[0].append(hi)
        parts[1].append(mid)
        parts[2].append(rest - mid)
    tiles = parts[0] + parts[0] + parts[1] + parts[1] + parts[2]
    tiles.append(jnp.zeros((8, 128), F32))
    return jnp.concatenate(tiles, axis=0).T


def turn_block(src, dt_ref, left_ref, right_ref):
    for plane in range(8):
        out = turned(src, plane)
        dt_ref[plane, 8:136] = out
        left_ref[plane] = out[0:8]
        right_ref[plane] = out[120:128]
    dt_ref[:, 0:8, :] = jnp.zeros((8, 8, 128), F32)
    dt_ref[:, 136:144, :] = jnp.zeros((8, 8, 128), F32)


def turn_kernel(down_ref, lup_ref, rup_ref, lown_ref, rown_ref, dt_ref, left_ref, right_ref):
    turn_block(down_ref, dt_ref, left_ref.at[16:24], right_ref.at[16:24])
    left_ref[0:8] = lup_ref[...]
    right_ref[0:8] = rup_ref[...]
    left_ref[8:16] = lown_ref[...]
    right_ref[8:16] = rown_ref[...]


def window_columns(dt_ref, lhs_ref, groups):
    for g in range(groups):
        for half in range(2):
            lhs_ref[half, g * 64 : (g + 1) * 64, :] = jnp.concatenate(
                [dt_ref[g, pl.ds(7 + 2 * half + j, 64, stride=2)] for j in range(2)], axis=1
            ).astype(BF)


def lift(lhs_ref, wl_ref, groups, pairs, dtype, store):
    for t in range(4):
        for half in range(2):
            out = leaky(mm(lhs_ref[half], wl_ref[t])).astype(BF).astype(dtype)
            out = out.reshape(groups, pairs, 256)
            for g in range(groups):
                for r in range(2):
                    store(
                        g,
                        2 * t + r,
                        slice(half * 128, (half + 1) * 128),
                        out[g, :, r * 128 : (r + 1) * 128],
                    )


PAIRS = (
    (0, 1, (1, 2, 3)),
    (1, 1, (0, 1, 2, 3)),
    (2, 1, (0, 1, 2, 3)),
    (3, 1, (0, 1, 2)),
)


def conv1(lhs_of, w1_ref, taps):
    weight = w1_ref[taps[0] * 3 : taps[-1] * 3 + 3].reshape(len(taps) * 768, 256)
    lhs = jnp.concatenate(
        [lhs_of((dp - 1) // 2, (dp + 1) % 2, b) for dp in taps for b in range(3)], axis=1
    ).astype(BF)
    return leaky(mm(lhs, weight)).astype(BF)


def conv1_rows(x4_ref, w1_ref, fn_ref, first, rows):
    for pp, n, taps in PAIRS:
        out = conv1(
            lambda h, s, b: x4_ref[
                pp + h : pp + h + n, s, first + b : first + b + rows
            ].reshape(n * rows * 64, 256),
            w1_ref,
            taps,
        )
        for q in range(2):
            fn_ref[pp : pp + n, q] = out[:, q * 128 : (q + 1) * 128].reshape(n, rows, 64, 128)


def reduce1(taps, wr1_ref):
    lhs = jnp.concatenate(taps, axis=1).astype(BF)
    return leaky(mm(lhs, wr1_ref[...])).astype(BF)


def own_kernel(
    own_hbm, lift_hbm, c1_hbm, x4b_ref, fn_ref, lown_ref, rown_ref, wl_ref, w1_ref,
    dt_ref, lhs_ref, x4_ref, own_ref, lift_ref, c1_ref, sems,
):
    copies = [
        pltpu.make_async_copy(src, dst, sems.at[n])
        for n, (src, dst) in enumerate(
            ((own_hbm, own_ref), (lift_hbm, lift_ref), (c1_hbm, c1_ref))
        )
    ]
    for copy in copies:
        copy.start()
    copies[0].wait()
    turn_block(own_ref, dt_ref, lown_ref, rown_ref)
    copies[1].wait()
    lift_weights(lift_ref, wl_ref)
    copies[2].wait()
    conv1_weights(c1_ref, w1_ref)
    window_columns(dt_ref, lhs_ref, 8)

    def store(g, row, lanes, values):
        x4_ref[g // 2, g % 2, row, :, lanes] = values
        if row in (0, 1, 6, 7):
            x4b_ref[g, row if row < 2 else row - 4, :, lanes] = values

    lift(lhs_ref, wl_ref, 8, 64, BF, store)
    conv1_rows(x4_ref, w1_ref, fn_ref, 0, 6)


def top_kernel(up_ref, x4b_ref, wl_ref, w1_ref, fn_ref, lup_ref, rup_ref, dt_ref, lhs_ref, x4_ref):
    turn_block(up_ref, dt_ref, lup_ref, rup_ref)
    window_columns(dt_ref, lhs_ref, 8)

    def store(g, row, lanes, values):
        x4_ref[g // 2, g % 2, row, :, lanes] = values

    lift(lhs_ref, wl_ref, 8, 64, BF, store)
    for plane in range(8):
        x4_ref[plane // 2, plane % 2, 8:10] = x4b_ref[plane, 0:2]
    conv1_rows(x4_ref, w1_ref, fn_ref, 1, 7)


def bottom_kernel(
    dt_ref, x4b_ref, fnt_ref, fno_ref, wl_ref, w1_ref, wr1_ref, fn_ref, mid_ref, lhs_ref, x4_ref
):
    window_columns(dt_ref, lhs_ref, 8)

    def store(g, row, lanes, values):
        x4_ref[g // 2, g % 2, row + 2, :, lanes] = values

    lift(lhs_ref, wl_ref, 8, 64, BF, store)
    for plane in range(8):
        x4_ref[plane // 2, plane % 2, 0:2] = x4b_ref[plane, 2:4]
    conv1_rows(x4_ref, w1_ref, fn_ref, 0, 7)
    for pp in range(4):

        def row_of(a, row):
            if row < 7:
                return fnt_ref[pp, a, row]
            if row < 13:
                return fno_ref[pp, a, row - 7]
            return fn_ref[pp, a, row - 13]

        taps = [
            jnp.concatenate([row_of(a, 2 * rr + b) for rr in range(10)], axis=0)
            for a in range(2)
            for b in range(2)
        ]
        mid_ref[pp] = reduce1(taps, wr1_ref).reshape(10, 64, 128)


def outer_kernel(
    lrecv_ref, left_ref, right_ref, rrecv_ref, wl_ref, w1_ref, wr1_ref, main_ref, wr2_ref, w3_ref, c2_hbm,
    edge_ref, skip_ref, chunk_ref,
    de_ref, dw_ref, lhs_ref, x4_ref, fn_ref, me_ref, mf_ref, xm_ref, ms_ref, cf_ref, w2_ref, sem,
):
    copies = [
        pltpu.make_async_copy(
            c2_hbm, w2_ref.at[3 * q : 3 * q + 9, :, q * 128 : (q + 1) * 128], sem.at[q]
        )
        for q in range(2)
    ]
    for copy in copies:
        copy.start()
    w2_ref[0:3, :, 128:256] = jnp.zeros((3, 384, 128), BF)
    w2_ref[9:12, :, 0:128] = jnp.zeros((3, 384, 128), BF)
    de_ref[:, 0:8] = lrecv_ref[...]
    de_ref[:, 8:16] = left_ref[...]
    de_ref[:, 16:24] = right_ref[...]
    de_ref[:, 24:32] = rrecv_ref[...]
    for half in range(2):
        dw_ref[half, :, 0:8] = de_ref[:, 1 + 2 * half : 9 + 2 * half]
        dw_ref[half, :, 8:16] = de_ref[:, 21 + 2 * half : 29 + 2 * half]
    for half in range(2):
        for g in range(0, 24, 2):
            lhs_ref[half, g * 8 : (g + 2) * 8, :] = jnp.concatenate(
                [
                    jnp.concatenate(
                        [dw_ref[half, g + k, pl.ds(j, 8, stride=2)] for k in range(2)], axis=0
                    )
                    for j in range(2)
                ],
                axis=1,
            ).astype(BF)

    zero = jnp.zeros((24, 8, 256), F32)
    x4_ref[0, 1] = zero
    x4_ref[5, 0] = zero

    def store(g, row, lanes, values):
        x4_ref[1 + g % 8 // 2, g % 2, g // 8 * 8 + row, :, lanes] = values

    lift(lhs_ref, wl_ref, 24, 8, F32, store)
    out = conv1(
        lambda h, s, b: x4_ref[1 + h : 5 + h, s, 1 + b : 21 + b].reshape(640, 256),
        w1_ref,
        range(4),
    ).astype(F32)
    for q in range(2):
        fn_ref[:, q] = out[:, q * 128 : (q + 1) * 128].reshape(4, 10, 2, 8, 128)
    edge_ref[...] = fn_ref[:, :, 3:7].reshape(8, 8, 8, 128)
    taps = [fn_ref[:, a, :, b].reshape(320, 128) for a in range(2) for b in range(2)]
    me_ref[...] = reduce1(taps, wr1_ref).astype(F32).reshape(4, 10, 8, 128)

    for n in range(40):
        plane, row = n // 10, n % 10
        mf_ref[n, 16:80] = main_ref[plane, row].astype(F32)
        mf_ref[n, 13:17] = me_ref[plane, row, 0:4]
        mf_ref[n, 79:83] = me_ref[plane, row, 4:8]
        for c in range(3):
            xm_ref[plane, row, :, c * 128 : (c + 1) * 128] = mf_ref[n, 7 + c : 87 + c].astype(BF)
    for copy in copies:
        copy.wait()
    for half in range(2):
        taps = range(1, 4) if half == 0 else range(0, 3)
        lhs = jnp.concatenate(
            [
                xm_ref[2 * half - 1 + dp, b : b + 8].reshape(640, 384)
                for dp in taps
                for b in range(3)
            ],
            axis=1,
        )
        weight = w2_ref[taps[0] * 3 : taps[0] * 3 + 9].reshape(3456, 256)
        out = rounded(leaky(mm(lhs, weight)))
        for q in range(2):
            ms_ref[2 * half + q, :, 0:80] = out[:, q * 128 : (q + 1) * 128].reshape(8, 80, 128)
    for plane in range(4):
        skip_ref[plane] = ms_ref[plane, 2:6, 8:72].astype(BF)
    taps = []
    for a in range(2):
        for b in range(2):
            for c in range(2):
                taps.append(
                    jnp.concatenate(
                        [
                            ms_ref[2 * plane + a, 2 * row + b, pl.ds(6 + c, 40, stride=2)]
                            for plane in range(2)
                            for row in range(4)
                        ],
                        axis=0,
                    )
                )
    lhs = jnp.concatenate(taps, axis=1).astype(BF)
    out = rounded(leaky(mm(lhs, wr2_ref[...])))
    cf_ref[...] = out.reshape(2, 4, 40, 256)
    lhs = []
    for plane in range(2):
        lhs.append(
            jnp.concatenate(
                [
                    jnp.concatenate(
                        [cf_ref[plane, row + b, c : c + 32] for row in range(2)], axis=0
                    )
                    for b in range(3)
                    for c in range(3)
                ],
                axis=1,
            ).astype(BF)
        )
    same = mm(jnp.concatenate(lhs, axis=0), w3_ref[1])
    first = same[0:64] + mm(lhs[1], w3_ref[2])
    second = same[64:128] + mm(lhs[0], w3_ref[0])
    out = jnp.concatenate([first[0:32], second[0:32], first[32:64], second[32:64]], axis=0)
    out = leaky(out).T
    chunk_ref[...] = out.reshape(64, 4, 128).astype(BF)


def finest_kernel(fnt_ref, fno_ref, fnb_ref, edge_ref, out_ref, wide_ref, rows_ref):
    lane = lax.broadcasted_iota(jnp.int32, (64, 128), 1)
    pair = lax.broadcasted_iota(jnp.int32, (64, 128), 0)
    for row in range(0, 8, 2):
        now = []
        for r in (row, row + 1):
            v = (fnt_ref[0, 0] if r == 0 else fnb_ref[0, 0] if r == 7 else fno_ref[0, r - 1]).astype(F32)
            v = jnp.where(pair == 0, edge_ref[0, r, 3:4], v)
            now.append(jnp.where(pair == 63, edge_ref[0, r, 4:5], v))
        wide_ref[row // 2, pl.ds(0, 64, stride=2), :] = jnp.where(
            lane < 64, now[0], pltpu.roll(now[1], 64, 1)
        )
        wide_ref[row // 2, pl.ds(1, 64, stride=2), :] = jnp.where(
            lane < 64, pltpu.roll(now[0], 64, 1), now[1]
        )
        turned = wide_ref[row // 2].T
        rows_ref[:, row, :] = turned[0:64]
        rows_ref[:, row + 1, :] = turned[64:128]
    out_ref[:, 0] = rows_ref[...].astype(BF)


def coarse_kernel(in_ref, out_ref, y_ref):
    all_in = in_ref[...].astype(F32)
    for c in range(4):
        v = all_in[:, c, :]
        y_ref[c, pl.ds(0, 64, stride=2), :] = v
        y_ref[c, pl.ds(1, 64, stride=2), :] = pltpu.roll(v, 64, 1)
    for c in range(4):
        out_ref[c] = y_ref[c].T[0:64].reshape(2, 32, 128).astype(BF)


def shift(array, axis, step):
    peers = lax.axis_size(axis)
    return lax.ppermute(array, axis, [(i, (i + step) % peers) for i in range(peers)])


def struct(shape, dtype):
    return jax.ShapeDtypeStruct(shape, dtype)


def on_device(disp, lift_w, conv1_w, reduce1_w, conv2_w, reduce2_w, conv3_w):
    own = disp.reshape(24, 8, 128)
    up = shift(own, "wide", 1)
    strip = struct((8, 8, 128), F32)
    fine_scratch = (VMEM((2, 512, 256), BF), VMEM((4, 2, 10, 64, 256), BF))
    turn_scratch = (VMEM((8, 144, 128), F32),)
    stay = lambda x: pltpu.with_memory_space_constraint(x, pltpu.HBM)
    x4b, fno, lown, rown, wl, w1 = call(
        own_kernel,
        (
            struct((8, 4, 64, 256), BF),
            struct((4, 2, 6, 64, 128), BF),
            strip,
            strip,
            struct((4, 256, 256), BF),
            struct((12, 256, 256), BF),
        ),
        (stay(own), stay(lift_w), stay(conv1_w.reshape(9, 192, 64))),
        14,
        scratch=turn_scratch
        + fine_scratch
        + (
            VMEM((24, 8, 128), F32),
            VMEM((3, 64), F32),
            VMEM((9, 192, 64), BF),
            pltpu.SemaphoreType.DMA((3,)),
        ),
        name="fine_own_rows",
        flops=2 * 10**9,
        nbytes=6 * 10**6,
        space=pltpu.HBM,
    )
    again, x4b = lax.optimization_barrier((own, x4b))
    down = shift(again, "wide", -1)
    fnt, lup, rup = call(
        top_kernel,
        (struct((4, 2, 7, 64, 128), BF), strip, strip),
        (up, x4b, wl, w1),
        12,
        scratch=turn_scratch + fine_scratch,
        name="fine_top_rows",
        flops=3 * 10**9,
        nbytes=6 * 10**6,
    )
    dt, left, right = call(
        turn_kernel,
        (struct((8, 144, 128), F32), struct((24, 8, 128), F32), struct((24, 8, 128), F32)),
        (down, lup, rup, lown, rown),
        6,
        name="columns_to_rows",
        flops=10**7,
        nbytes=2 * 10**6,
    )
    rrecv = shift(left, "narrow", -1)
    lrecv = shift(right, "narrow", 1)
    wr1 = reduce1_w.reshape(512, 128)
    fnb, mid = call(
        bottom_kernel,
        (struct((4, 2, 7, 64, 128), BF), struct((4, 10, 64, 128), BF)),
        (dt, x4b, fnt, fno, wl, w1, wr1),
        14,
        scratch=fine_scratch,
        name="fine_bottom_rows",
        flops=8 * 10**9,
        nbytes=6 * 10**6,
    )
    edge, skip, chunk = call(
        outer_kernel,
        (struct((8, 8, 8, 128), F32), struct((4, 4, 64, 128), BF), struct((64, 4, 128), BF)),
        (
            lrecv, left, right, rrecv, wl, w1, wr1, mid,
            reduce2_w.reshape(1024, 256), conv3_w.reshape(3, 2304, 256),
            stay(conv2_w.reshape(9, 384, 128)),
        ),
        26,
        last=pltpu.HBM,
        scratch=(
            VMEM((24, 32, 128), F32),
            VMEM((2, 24, 16, 128), F32),
            VMEM((2, 192, 256), BF),
            VMEM((6, 2, 24, 8, 256), F32),
            VMEM((4, 2, 10, 2, 8, 128), F32),
            VMEM((4, 10, 8, 128), F32),
            VMEM((40, 96, 128), F32),
            VMEM((4, 10, 80, 384), BF),
            VMEM((4, 8, 88, 128), F32),
            VMEM((2, 4, 40, 256), F32),
            VMEM((12, 384, 256), BF),
            pltpu.SemaphoreType.DMA((2,)),
        ),
        name="middle_and_coarse",
        flops=6 * 10**9,
        nbytes=12 * 10**6,
    )
    received = lax.all_to_all(chunk, "wide", 0, 0, tiled=True)
    finest = pl.pallas_call(
        finest_kernel,
        grid=(8,),
        out_shape=struct((64, 8, 8, 128), BF),
        in_specs=[
            pl.BlockSpec((1, 1, 64, 128), lambda p: (p, 6, 0, 0)),
            pl.BlockSpec((1, 6, 64, 128), lambda p: (p, 0, 0, 0)),
            pl.BlockSpec((1, 1, 64, 128), lambda p: (p, 0, 0, 0)),
            pl.BlockSpec((1, 8, 8, 128), lambda p: (p, 0, 0, 0)),
        ],
        out_specs=pl.BlockSpec((64, 1, 8, 128), lambda p: (0, p, 0, 0)),
        scratch_shapes=[VMEM((4, 128, 128), F32), VMEM((64, 8, 128), F32)],
        compiler_params=pltpu.CompilerParams(vmem_limit_bytes=6 * MIB),
        cost_estimate=pl.CostEstimate(flops=10**8, bytes_accessed=3 * 10**6, transcendentals=0),
        name="finest_layout",
    )(
        fnt.reshape(8, 7, 64, 128),
        fno.reshape(8, 6, 64, 128),
        fnb.reshape(8, 7, 64, 128),
        edge,
    )
    coarse = call(
        coarse_kernel,
        struct((4, 2, 32, 128), BF),
        (received,),
        4,
        scratch=(VMEM((4, 128, 128), F32),),
        name="coarse_layout",
        flops=10**6,
        nbytes=2 * 10**5,
    )
    return finest, skip.transpose(3, 0, 1, 2), coarse.transpose(0, 1, 3, 2)


def solution(mesh):
    return jax.shard_map(
        on_device,
        mesh=mesh,
        in_specs=(P(None, None, "wide", "narrow"), P(), P(), P(), P(), P(), P()),
        out_specs=(
            P(None, None, "wide", "narrow"),
            P(None, None, "wide", "narrow"),
            P("wide", None, None, "narrow"),
        ),
        check_vma=False,
    )
```

```python
import jax
import jax.numpy as jnp
from jax import lax
from jax.experimental import pallas as pl
from jax.experimental.pallas import tpu as pltpu
from jax.sharding import PartitionSpec as P

F32 = jnp.float32
BF = jnp.bfloat16
VMEM = pltpu.VMEM
MIB = 1024 * 1024


def leaky(v):
    return jnp.maximum(v, 0.01 * v)


def rounded(v):
    return v.astype(BF).astype(F32)


def mm(a, b):
    return jnp.dot(a, b, preferred_element_type=F32)


def call(kernel, outs, args, limit, scratch=(), name=None, flops=0, nbytes=0, space=VMEM, last=None):
    whole = pl.BlockSpec(memory_space=VMEM)
    return pl.pallas_call(
        kernel,
        out_shape=outs,
        in_specs=[pl.BlockSpec(memory_space=space)] * (len(args) - 1)
        + [pl.BlockSpec(memory_space=last or space)],
        out_specs=jax.tree.map(lambda _: whole, outs),
        scratch_shapes=list(scratch),
        compiler_params=pltpu.CompilerParams(vmem_limit_bytes=limit * MIB),
        cost_estimate=pl.CostEstimate(flops=flops, bytes_accessed=nbytes, transcendentals=0),
        name=name,
    )(*args)


def lift_weights(lift_ref, wl_ref):
    w = lift_ref[...]
    hi = rounded(w)
    low = rounded(w - hi)
    place = (
        lax.broadcasted_iota(jnp.int32, (64, 256), 1) % 64
        == lax.broadcasted_iota(jnp.int32, (64, 256), 0)
    ).astype(BF)
    hi4 = mm(hi.astype(BF), place)
    low4 = mm(low.astype(BF), place)
    terms = []
    for s in range(5):
        for m in range(3):
            src = low4 if s in (1, 3) else hi4
            terms.append(jnp.broadcast_to(src[m : m + 1, :], (8, 256)))
    terms.append(jnp.zeros((8, 256), F32))
    base = jnp.concatenate(terms, axis=0)
    row = lax.broadcasted_iota(jnp.int32, (128, 256), 0) % 8
    lane = lax.broadcasted_iota(jnp.int32, (128, 256), 1)
    for t in range(4):
        for j in range(2):
            keep = (row == 2 * t + lane // 128) & (lane // 64 % 2 == j)
            wl_ref[t, j * 128 : (j + 1) * 128, :] = jnp.where(keep, base, 0.0).astype(BF)


def conv1_weights(c1_ref, w1_ref):
    rows64 = lax.broadcasted_iota(jnp.int32, (64, 128), 0)
    lanes64 = lax.broadcasted_iota(jnp.int32, (64, 128), 1)
    left = (rows64 == lanes64).astype(BF)
    right = (rows64 + 64 == lanes64).astype(BF)
    zero1 = jnp.zeros((256, 128), BF)
    zero64 = jnp.zeros((64, 128), F32)
    for b in range(3):
        for a in range(3):
            k = c1_ref[a * 3 + b]
            pair = jnp.concatenate([mm(k, left), zero64], 0) + jnp.concatenate(
                [zero64, mm(k, right)], 0
            )
            pair = pair.astype(BF)
            w1_ref[a * 3 + b, :, 0:128] = pair
            w1_ref[(a + 1) * 3 + b, :, 128:256] = pair
        w1_ref[9 + b, :, 0:128] = zero1
        w1_ref[b, :, 128:256] = zero1


def turned(src, plane):
    parts = [[], [], []]
    for m in range(3):
        v = src[m * 8 + plane]
        hi = rounded(v)
        rest = v - hi
        mid = rounded(rest)
        parts[0].append(hi)
        parts[1].append(mid)
        parts[2].append(rest - mid)
    tiles = parts[0] + parts[0] + parts[1] + parts[1] + parts[2]
    tiles.append(jnp.zeros((8, 128), F32))
    return jnp.concatenate(tiles, axis=0).T


def turn_block(src, dt_ref, left_ref, right_ref):
    for plane in range(8):
        out = turned(src, plane)
        dt_ref[plane, 8:136] = out
        left_ref[plane] = out[0:8]
        right_ref[plane] = out[120:128]
    dt_ref[:, 0:8, :] = jnp.zeros((8, 8, 128), F32)
    dt_ref[:, 136:144, :] = jnp.zeros((8, 8, 128), F32)


def turn_kernel(down_ref, lup_ref, rup_ref, lown_ref, rown_ref, dt_ref, left_ref, right_ref):
    turn_block(down_ref, dt_ref, left_ref.at[16:24], right_ref.at[16:24])
    left_ref[0:8] = lup_ref[...]
    right_ref[0:8] = rup_ref[...]
    left_ref[8:16] = lown_ref[...]
    right_ref[8:16] = rown_ref[...]


def window_columns(dt_ref, lhs_ref, groups):
    for g in range(groups):
        for half in range(2):
            lhs_ref[half, g * 64 : (g + 1) * 64, :] = jnp.concatenate(
                [dt_ref[g, pl.ds(7 + 2 * half + j, 64, stride=2)] for j in range(2)], axis=1
            ).astype(BF)


def lift(lhs_ref, wl_ref, groups, pairs, dtype, store):
    for t in range(4):
        for half in range(2):
            out = leaky(mm(lhs_ref[half], wl_ref[t])).astype(BF).astype(dtype)
            out = out.reshape(groups, pairs, 256)
            for g in range(groups):
                for r in range(2):
                    store(
                        g,
                        2 * t + r,
                        slice(half * 128, (half + 1) * 128),
                        out[g, :, r * 128 : (r + 1) * 128],
                    )


PAIRS = (
    (0, 1, (1, 2, 3)),
    (1, 1, (0, 1, 2, 3)),
    (2, 1, (0, 1, 2, 3)),
    (3, 1, (0, 1, 2)),
)


def conv1(lhs_of, w1_ref, taps):
    weight = w1_ref[taps[0] * 3 : taps[-1] * 3 + 3].reshape(len(taps) * 768, 256)
    lhs = jnp.concatenate(
        [lhs_of((dp - 1) // 2, (dp + 1) % 2, b) for dp in taps for b in range(3)], axis=1
    ).astype(BF)
    return leaky(mm(lhs, weight)).astype(BF)


def conv1_rows(x4_ref, w1_ref, fn_ref, first, rows):
    for pp, n, taps in PAIRS:
        out = conv1(
            lambda h, s, b: x4_ref[
                pp + h : pp + h + n, s, first + b : first + b + rows
            ].reshape(n * rows * 64, 256),
            w1_ref,
            taps,
        )
        for q in range(2):
            fn_ref[pp : pp + n, q] = out[:, q * 128 : (q + 1) * 128].reshape(n, rows, 64, 128)


def reduce1(taps, wr1_ref):
    lhs = jnp.concatenate(taps, axis=1).astype(BF)
    return leaky(mm(lhs, wr1_ref[...])).astype(BF)


def own_kernel(
    own_hbm, lift_hbm, c1_hbm, x4_ref, lown_ref, rown_ref, wl_ref, w1_ref,
    dt_ref, lhs_ref, own_ref, lift_ref, c1_ref, sems,
):
    copies = [
        pltpu.make_async_copy(src, dst, sems.at[n])
        for n, (src, dst) in enumerate(
            ((own_hbm, own_ref), (lift_hbm, lift_ref), (c1_hbm, c1_ref))
        )
    ]
    for copy in copies:
        copy.start()
    copies[0].wait()
    turn_block(own_ref, dt_ref, lown_ref, rown_ref)
    copies[1].wait()
    lift_weights(lift_ref, wl_ref)
    copies[2].wait()
    conv1_weights(c1_ref, w1_ref)
    window_columns(dt_ref, lhs_ref, 8)

    def store(g, row, lanes, values):
        x4_ref[g // 2, g % 2, row, :, lanes] = values

    lift(lhs_ref, wl_ref, 8, 64, BF, store)


def own_rows_kernel(x4_ref, w1_ref, fn_ref):
    conv1_rows(x4_ref, w1_ref, fn_ref, 0, 6)


def top_kernel(up_ref, x4b_ref, wl_ref, w1_ref, fn_ref, lup_ref, rup_ref, dt_ref, lhs_ref, x4_ref):
    turn_block(up_ref, dt_ref, lup_ref, rup_ref)
    window_columns(dt_ref, lhs_ref, 8)

    def store(g, row, lanes, values):
        x4_ref[g // 2, g % 2, row, :, lanes] = values

    lift(lhs_ref, wl_ref, 8, 64, BF, store)
    for plane in range(8):
        x4_ref[plane // 2, plane % 2, 8:10] = x4b_ref[plane // 2, plane % 2, 0:2]
    conv1_rows(x4_ref, w1_ref, fn_ref, 1, 7)


def bottom_kernel(
    dt_ref, x4b_ref, fnt_ref, fno_ref, wl_ref, w1_ref, wr1_ref, fn_ref, mid_ref, lhs_ref, x4_ref
):
    window_columns(dt_ref, lhs_ref, 8)

    def store(g, row, lanes, values):
        x4_ref[g // 2, g % 2, row + 2, :, lanes] = values

    lift(lhs_ref, wl_ref, 8, 64, BF, store)
    for plane in range(8):
        x4_ref[plane // 2, plane % 2, 0:2] = x4b_ref[plane // 2, plane % 2, 6:8]
    conv1_rows(x4_ref, w1_ref, fn_ref, 0, 7)
    for pp in range(4):

        def row_of(a, row):
            if row < 7:
                return fnt_ref[pp, a, row]
            if row < 13:
                return fno_ref[pp, a, row - 7]
            return fn_ref[pp, a, row - 13]

        taps = [
            jnp.concatenate([row_of(a, 2 * rr + b) for rr in range(10)], axis=0)
            for a in range(2)
            for b in range(2)
        ]
        mid_ref[pp] = reduce1(taps, wr1_ref).reshape(10, 64, 128)


def outer_kernel(
    lrecv_ref, left_ref, right_ref, rrecv_ref, wl_ref, w1_ref, wr1_ref, main_ref, wr2_ref, w3_ref, c2_hbm,
    edge_ref, skip_ref, chunk_ref,
    de_ref, dw_ref, lhs_ref, x4_ref, fn_ref, me_ref, mf_ref, xm_ref, ms_ref, cf_ref, w2_ref, sem,
):
    copies = [
        pltpu.make_async_copy(
            c2_hbm, w2_ref.at[3 * q : 3 * q + 9, :, q * 128 : (q + 1) * 128], sem.at[q]
        )
        for q in range(2)
    ]
    for copy in copies:
        copy.start()
    w2_ref[0:3, :, 128:256] = jnp.zeros((3, 384, 128), BF)
    w2_ref[9:12, :, 0:128] = jnp.zeros((3, 384, 128), BF)
    de_ref[:, 0:8] = lrecv_ref[...]
    de_ref[:, 8:16] = left_ref[...]
    de_ref[:, 16:24] = right_ref[...]
    de_ref[:, 24:32] = rrecv_ref[...]
    for half in range(2):
        dw_ref[half, :, 0:8] = de_ref[:, 1 + 2 * half : 9 + 2 * half]
        dw_ref[half, :, 8:16] = de_ref[:, 21 + 2 * half : 29 + 2 * half]
    for half in range(2):
        for g in range(0, 24, 2):
            lhs_ref[half, g * 8 : (g + 2) * 8, :] = jnp.concatenate(
                [
                    jnp.concatenate(
                        [dw_ref[half, g + k, pl.ds(j, 8, stride=2)] for k in range(2)], axis=0
                    )
                    for j in range(2)
                ],
                axis=1,
            ).astype(BF)

    zero = jnp.zeros((24, 8, 256), F32)
    x4_ref[0, 1] = zero
    x4_ref[5, 0] = zero

    def store(g, row, lanes, values):
        x4_ref[1 + g % 8 // 2, g % 2, g // 8 * 8 + row, :, lanes] = values

    lift(lhs_ref, wl_ref, 24, 8, F32, store)
    out = conv1(
        lambda h, s, b: x4_ref[1 + h : 5 + h, s, 1 + b : 21 + b].reshape(640, 256),
        w1_ref,
        range(4),
    ).astype(F32)
    for q in range(2):
        fn_ref[:, q] = out[:, q * 128 : (q + 1) * 128].reshape(4, 10, 2, 8, 128)
    edge_ref[...] = fn_ref[:, :, 3:7].reshape(8, 8, 8, 128)
    taps = [fn_ref[:, a, :, b].reshape(320, 128) for a in range(2) for b in range(2)]
    me_ref[...] = reduce1(taps, wr1_ref).astype(F32).reshape(4, 10, 8, 128)

    for n in range(40):
        plane, row = n // 10, n % 10
        mf_ref[n, 16:80] = main_ref[plane, row].astype(F32)
        mf_ref[n, 13:17] = me_ref[plane, row, 0:4]
        mf_ref[n, 79:83] = me_ref[plane, row, 4:8]
        for c in range(3):
            xm_ref[plane, row, :, c * 128 : (c + 1) * 128] = mf_ref[n, 7 + c : 87 + c].astype(BF)
    for copy in copies:
        copy.wait()
    for half in range(2):
        taps = range(1, 4) if half == 0 else range(0, 3)
        lhs = jnp.concatenate(
            [
                xm_ref[2 * half - 1 + dp, b : b + 8].reshape(640, 384)
                for dp in taps
                for b in range(3)
            ],
            axis=1,
        )
        weight = w2_ref[taps[0] * 3 : taps[0] * 3 + 9].reshape(3456, 256)
        out = rounded(leaky(mm(lhs, weight)))
        for q in range(2):
            ms_ref[2 * half + q, :, 0:80] = out[:, q * 128 : (q + 1) * 128].reshape(8, 80, 128)
    for plane in range(4):
        skip_ref[plane] = ms_ref[plane, 2:6, 8:72].astype(BF)
    taps = []
    for a in range(2):
        for b in range(2):
            for c in range(2):
                taps.append(
                    jnp.concatenate(
                        [
                            ms_ref[2 * plane + a, 2 * row + b, pl.ds(6 + c, 40, stride=2)]
                            for plane in range(2)
                            for row in range(4)
                        ],
                        axis=0,
                    )
                )
    lhs = jnp.concatenate(taps, axis=1).astype(BF)
    out = rounded(leaky(mm(lhs, wr2_ref[...])))
    cf_ref[...] = out.reshape(2, 4, 40, 256)
    lhs = []
    for plane in range(2):
        lhs.append(
            jnp.concatenate(
                [
                    jnp.concatenate(
                        [cf_ref[plane, row + b, c : c + 32] for row in range(2)], axis=0
                    )
                    for b in range(3)
                    for c in range(3)
                ],
                axis=1,
            ).astype(BF)
        )
    same = mm(jnp.concatenate(lhs, axis=0), w3_ref[1])
    first = same[0:64] + mm(lhs[1], w3_ref[2])
    second = same[64:128] + mm(lhs[0], w3_ref[0])
    out = jnp.concatenate([first[0:32], second[0:32], first[32:64], second[32:64]], axis=0)
    out = leaky(out).T
    chunk_ref[...] = out.reshape(64, 4, 128).astype(BF)


def finest_kernel(fnt_ref, fno_ref, fnb_ref, edge_ref, out_ref, wide_ref, rows_ref):
    lane = lax.broadcasted_iota(jnp.int32, (64, 128), 1)
    pair = lax.broadcasted_iota(jnp.int32, (64, 128), 0)
    for row in range(0, 8, 2):
        now = []
        for r in (row, row + 1):
            v = (fnt_ref[0, 0] if r == 0 else fnb_ref[0, 0] if r == 7 else fno_ref[0, r - 1]).astype(F32)
            v = jnp.where(pair == 0, edge_ref[0, r, 3:4], v)
            now.append(jnp.where(pair == 63, edge_ref[0, r, 4:5], v))
        wide_ref[row // 2, pl.ds(0, 64, stride=2), :] = jnp.where(
            lane < 64, now[0], pltpu.roll(now[1], 64, 1)
        )
        wide_ref[row // 2, pl.ds(1, 64, stride=2), :] = jnp.where(
            lane < 64, pltpu.roll(now[0], 64, 1), now[1]
        )
        turned = wide_ref[row // 2].T
        rows_ref[:, row, :] = turned[0:64]
        rows_ref[:, row + 1, :] = turned[64:128]
    out_ref[:, 0] = rows_ref[...].astype(BF)


def coarse_kernel(in_ref, out_ref, y_ref):
    all_in = in_ref[...].astype(F32)
    for c in range(4):
        v = all_in[:, c, :]
        y_ref[c, pl.ds(0, 64, stride=2), :] = v
        y_ref[c, pl.ds(1, 64, stride=2), :] = pltpu.roll(v, 64, 1)
    for c in range(4):
        out_ref[c] = y_ref[c].T[0:64].reshape(2, 32, 128).astype(BF)


def shift(array, axis, step):
    peers = lax.axis_size(axis)
    return lax.ppermute(array, axis, [(i, (i + step) % peers) for i in range(peers)])


def struct(shape, dtype):
    return jax.ShapeDtypeStruct(shape, dtype)


def on_device(disp, lift_w, conv1_w, reduce1_w, conv2_w, reduce2_w, conv3_w):
    own = disp.reshape(24, 8, 128)
    up = shift(own, "wide", 1)
    strip = struct((8, 8, 128), F32)
    fine_scratch = (VMEM((2, 512, 256), BF), VMEM((4, 2, 10, 64, 256), BF))
    turn_scratch = (VMEM((8, 144, 128), F32),)
    stay = lambda x: pltpu.with_memory_space_constraint(x, pltpu.HBM)
    x4b, lown, rown, wl, w1 = call(
        own_kernel,
        (
            struct((4, 2, 8, 64, 256), BF),
            strip,
            strip,
            struct((4, 256, 256), BF),
            struct((12, 256, 256), BF),
        ),
        (stay(own), stay(lift_w), stay(conv1_w.reshape(9, 192, 64))),
        14,
        scratch=turn_scratch
        + (
            VMEM((2, 512, 256), BF),
            VMEM((24, 8, 128), F32),
            VMEM((3, 64), F32),
            VMEM((9, 192, 64), BF),
            pltpu.SemaphoreType.DMA((3,)),
        ),
        name="fine_own_lift",
        flops=2 * 10**9,
        nbytes=6 * 10**6,
        space=pltpu.HBM,
    )
    again, x4b = lax.optimization_barrier((own, x4b))
    down = shift(again, "wide", -1)
    fnt, lup, rup = call(
        top_kernel,
        (struct((4, 2, 7, 64, 128), BF), strip, strip),
        (up, x4b, wl, w1),
        12,
        scratch=turn_scratch + fine_scratch,
        name="fine_top_rows",
        flops=3 * 10**9,
        nbytes=6 * 10**6,
    )
    dt, left, right = call(
        turn_kernel,
        (struct((8, 144, 128), F32), struct((24, 8, 128), F32), struct((24, 8, 128), F32)),
        (down, lup, rup, lown, rown),
        6,
        name="columns_to_rows",
        flops=10**7,
        nbytes=2 * 10**6,
    )
    rrecv = shift(left, "narrow", -1)
    fno = call(
        own_rows_kernel,
        struct((4, 2, 6, 64, 128), BF),
        (x4b, w1),
        8,
        name="fine_own_rows",
        flops=2 * 10**9,
        nbytes=6 * 10**6,
    )
    again, fno = lax.optimization_barrier((right, fno))
    lrecv = shift(again, "narrow", 1)
    dt, rrecv = lax.optimization_barrier((dt, rrecv))
    wr1 = reduce1_w.reshape(512, 128)
    fnb, mid = call(
        bottom_kernel,
        (struct((4, 2, 7, 64, 128), BF), struct((4, 10, 64, 128), BF)),
        (dt, x4b, fnt, fno, wl, w1, wr1),
        14,
        scratch=fine_scratch,
        name="fine_bottom_rows",
        flops=8 * 10**9,
        nbytes=6 * 10**6,
    )
    edge, skip, chunk = call(
        outer_kernel,
        (struct((8, 8, 8, 128), F32), struct((4, 4, 64, 128), BF), struct((64, 4, 128), BF)),
        (
            lrecv, left, right, rrecv, wl, w1, wr1, mid,
            reduce2_w.reshape(1024, 256), conv3_w.reshape(3, 2304, 256),
            stay(conv2_w.reshape(9, 384, 128)),
        ),
        26,
        last=pltpu.HBM,
        scratch=(
            VMEM((24, 32, 128), F32),
            VMEM((2, 24, 16, 128), F32),
            VMEM((2, 192, 256), BF),
            VMEM((6, 2, 24, 8, 256), F32),
            VMEM((4, 2, 10, 2, 8, 128), F32),
            VMEM((4, 10, 8, 128), F32),
            VMEM((40, 96, 128), F32),
            VMEM((4, 10, 80, 384), BF),
            VMEM((4, 8, 88, 128), F32),
            VMEM((2, 4, 40, 256), F32),
            VMEM((12, 384, 256), BF),
            pltpu.SemaphoreType.DMA((2,)),
        ),
        name="middle_and_coarse",
        flops=6 * 10**9,
        nbytes=12 * 10**6,
    )
    received = lax.all_to_all(chunk, "wide", 0, 0, tiled=True)
    finest = pl.pallas_call(
        finest_kernel,
        grid=(8,),
        out_shape=struct((64, 8, 8, 128), BF),
        in_specs=[
            pl.BlockSpec((1, 1, 64, 128), lambda p: (p, 6, 0, 0)),
            pl.BlockSpec((1, 6, 64, 128), lambda p: (p, 0, 0, 0)),
            pl.BlockSpec((1, 1, 64, 128), lambda p: (p, 0, 0, 0)),
            pl.BlockSpec((1, 8, 8, 128), lambda p: (p, 0, 0, 0)),
        ],
        out_specs=pl.BlockSpec((64, 1, 8, 128), lambda p: (0, p, 0, 0)),
        scratch_shapes=[VMEM((4, 128, 128), F32), VMEM((64, 8, 128), F32)],
        compiler_params=pltpu.CompilerParams(vmem_limit_bytes=6 * MIB),
        cost_estimate=pl.CostEstimate(flops=10**8, bytes_accessed=3 * 10**6, transcendentals=0),
        name="finest_layout",
    )(
        fnt.reshape(8, 7, 64, 128),
        fno.reshape(8, 6, 64, 128),
        fnb.reshape(8, 7, 64, 128),
        edge,
    )
    coarse = call(
        coarse_kernel,
        struct((4, 2, 32, 128), BF),
        (received,),
        4,
        scratch=(VMEM((4, 128, 128), F32),),
        name="coarse_layout",
        flops=10**6,
        nbytes=2 * 10**5,
    )
    return finest, skip.transpose(3, 0, 1, 2), coarse.transpose(0, 1, 3, 2)


def solution(mesh):
    return jax.shard_map(
        on_device,
        mesh=mesh,
        in_specs=(P(None, None, "wide", "narrow"), P(), P(), P(), P(), P(), P()),
        out_specs=(
            P(None, None, "wide", "narrow"),
            P(None, None, "wide", "narrow"),
            P("wide", None, None, "narrow"),
        ),
        check_vma=False,
    )
```

```python
import jax
import jax.numpy as jnp
from jax import lax
from jax.experimental import pallas as pl
from jax.experimental.pallas import tpu as pltpu
from jax.sharding import PartitionSpec as P

F32 = jnp.float32
BF = jnp.bfloat16
VMEM = pltpu.VMEM
MIB = 1024 * 1024


def leaky(v):
    return jnp.maximum(v, 0.01 * v)


def rounded(v):
    return v.astype(BF).astype(F32)


def mm(a, b):
    return jnp.dot(a, b, preferred_element_type=F32)


def call(kernel, outs, args, limit, scratch=(), name=None, flops=0, nbytes=0, space=VMEM, last=None):
    whole = pl.BlockSpec(memory_space=VMEM)
    return pl.pallas_call(
        kernel,
        out_shape=outs,
        in_specs=[pl.BlockSpec(memory_space=space)] * (len(args) - 1)
        + [pl.BlockSpec(memory_space=last or space)],
        out_specs=jax.tree.map(lambda _: whole, outs),
        scratch_shapes=list(scratch),
        compiler_params=pltpu.CompilerParams(vmem_limit_bytes=limit * MIB),
        cost_estimate=pl.CostEstimate(flops=flops, bytes_accessed=nbytes, transcendentals=0),
        name=name,
    )(*args)


def lift_weights(lift_ref, wl_ref):
    w = lift_ref[...]
    hi = rounded(w)
    low = rounded(w - hi)
    place = (
        lax.broadcasted_iota(jnp.int32, (64, 256), 1) % 64
        == lax.broadcasted_iota(jnp.int32, (64, 256), 0)
    ).astype(BF)
    hi4 = mm(hi.astype(BF), place)
    low4 = mm(low.astype(BF), place)
    terms = []
    for s in range(5):
        for m in range(3):
            src = low4 if s in (1, 3) else hi4
            terms.append(jnp.broadcast_to(src[m : m + 1, :], (8, 256)))
    terms.append(jnp.zeros((8, 256), F32))
    base = jnp.concatenate(terms, axis=0)
    row = lax.broadcasted_iota(jnp.int32, (128, 256), 0) % 8
    lane = lax.broadcasted_iota(jnp.int32, (128, 256), 1)
    for t in range(4):
        for j in range(2):
            keep = (row == 2 * t + lane // 128) & (lane // 64 % 2 == j)
            wl_ref[t, j * 128 : (j + 1) * 128, :] = jnp.where(keep, base, 0.0).astype(BF)


def conv1_weights(c1_ref, w1_ref):
    rows64 = lax.broadcasted_iota(jnp.int32, (64, 128), 0)
    lanes64 = lax.broadcasted_iota(jnp.int32, (64, 128), 1)
    left = (rows64 == lanes64).astype(BF)
    right = (rows64 + 64 == lanes64).astype(BF)
    zero1 = jnp.zeros((256, 128), BF)
    zero64 = jnp.zeros((64, 128), F32)
    for b in range(3):
        for a in range(3):
            k = c1_ref[a * 3 + b]
            pair = jnp.concatenate([mm(k, left), zero64], 0) + jnp.concatenate(
                [zero64, mm(k, right)], 0
            )
            pair = pair.astype(BF)
            w1_ref[a * 3 + b, :, 0:128] = pair
            w1_ref[(a + 1) * 3 + b, :, 128:256] = pair
        w1_ref[9 + b, :, 0:128] = zero1
        w1_ref[b, :, 128:256] = zero1


def turned(src, plane):
    parts = [[], [], []]
    for m in range(3):
        v = src[m * 8 + plane]
        hi = rounded(v)
        rest = v - hi
        mid = rounded(rest)
        parts[0].append(hi)
        parts[1].append(mid)
        parts[2].append(rest - mid)
    tiles = parts[0] + parts[0] + parts[1] + parts[1] + parts[2]
    tiles.append(jnp.zeros((8, 128), F32))
    return jnp.concatenate(tiles, axis=0).T


def turn_block(src, dt_ref, left_ref, right_ref):
    for plane in range(8):
        out = turned(src, plane)
        dt_ref[plane, 8:136] = out
        left_ref[plane] = out[0:8].astype(left_ref.dtype)
        right_ref[plane] = out[120:128].astype(right_ref.dtype)
    dt_ref[:, 0:8, :] = jnp.zeros((8, 8, 128), F32)
    dt_ref[:, 136:144, :] = jnp.zeros((8, 8, 128), F32)


def turn_kernel(down_ref, lup_ref, rup_ref, lown_ref, rown_ref, dt_ref, left_ref, right_ref):
    turn_block(down_ref, dt_ref, left_ref.at[16:24], right_ref.at[16:24])
    left_ref[0:8] = lup_ref[...].astype(BF)
    right_ref[0:8] = rup_ref[...].astype(BF)
    left_ref[8:16] = lown_ref[...].astype(BF)
    right_ref[8:16] = rown_ref[...].astype(BF)


def window_columns(dt_ref, lhs_ref, groups):
    for g in range(groups):
        for half in range(2):
            lhs_ref[half, g * 64 : (g + 1) * 64, :] = jnp.concatenate(
                [dt_ref[g, pl.ds(7 + 2 * half + j, 64, stride=2)] for j in range(2)], axis=1
            ).astype(BF)


def lift(lhs_ref, wl_ref, groups, pairs, dtype, store):
    for t in range(4):
        for half in range(2):
            out = leaky(mm(lhs_ref[half], wl_ref[t])).astype(BF).astype(dtype)
            out = out.reshape(groups, pairs, 256)
            for g in range(groups):
                for r in range(2):
                    store(
                        g,
                        2 * t + r,
                        slice(half * 128, (half + 1) * 128),
                        out[g, :, r * 128 : (r + 1) * 128],
                    )


PAIRS = (
    (0, 1, (1, 2, 3)),
    (1, 1, (0, 1, 2, 3)),
    (2, 1, (0, 1, 2, 3)),
    (3, 1, (0, 1, 2)),
)


def conv1(lhs_of, w1_ref, taps):
    weight = w1_ref[taps[0] * 3 : taps[-1] * 3 + 3].reshape(len(taps) * 768, 256)
    lhs = jnp.concatenate(
        [lhs_of((dp - 1) // 2, (dp + 1) % 2, b) for dp in taps for b in range(3)], axis=1
    ).astype(BF)
    return leaky(mm(lhs, weight)).astype(BF)


def conv1_rows(x4_ref, w1_ref, fn_ref, first, rows):
    for pp, n, taps in PAIRS:
        out = conv1(
            lambda h, s, b: x4_ref[
                pp + h : pp + h + n, s, first + b : first + b + rows
            ].reshape(n * rows * 64, 256),
            w1_ref,
            taps,
        )
        for q in range(2):
            fn_ref[pp : pp + n, q] = out[:, q * 128 : (q + 1) * 128].reshape(n, rows, 64, 128)


def reduce1(taps, wr1_ref):
    lhs = jnp.concatenate(taps, axis=1).astype(BF)
    return leaky(mm(lhs, wr1_ref[...])).astype(BF)


def own_kernel(
    own_hbm, lift_hbm, c1_hbm, x4_ref, lown_ref, rown_ref, wl_ref, w1_ref,
    dt_ref, lhs_ref, own_ref, lift_ref, c1_ref, sems,
):
    copies = [
        pltpu.make_async_copy(src, dst, sems.at[n])
        for n, (src, dst) in enumerate(
            ((own_hbm, own_ref), (lift_hbm, lift_ref), (c1_hbm, c1_ref))
        )
    ]
    for copy in copies:
        copy.start()
    copies[0].wait()
    turn_block(own_ref, dt_ref, lown_ref, rown_ref)
    copies[1].wait()
    lift_weights(lift_ref, wl_ref)
    copies[2].wait()
    conv1_weights(c1_ref, w1_ref)
    window_columns(dt_ref, lhs_ref, 8)

    def store(g, row, lanes, values):
        x4_ref[g // 2, g % 2, row, :, lanes] = values

    lift(lhs_ref, wl_ref, 8, 64, BF, store)


def own_rows_kernel(x4_ref, w1_ref, fn_ref):
    conv1_rows(x4_ref, w1_ref, fn_ref, 0, 6)


def top_kernel(up_ref, x4b_ref, wl_ref, w1_ref, fn_ref, lup_ref, rup_ref, dt_ref, lhs_ref, x4_ref):
    turn_block(up_ref, dt_ref, lup_ref, rup_ref)
    window_columns(dt_ref, lhs_ref, 8)

    def store(g, row, lanes, values):
        x4_ref[g // 2, g % 2, row, :, lanes] = values

    lift(lhs_ref, wl_ref, 8, 64, BF, store)
    for plane in range(8):
        x4_ref[plane // 2, plane % 2, 8:10] = x4b_ref[plane // 2, plane % 2, 0:2]
    conv1_rows(x4_ref, w1_ref, fn_ref, 1, 7)


def bottom_kernel(
    dt_ref, x4b_ref, fnt_ref, fno_ref, wl_ref, w1_ref, wr1_ref, fn_ref, mid_ref, lhs_ref, x4_ref
):
    window_columns(dt_ref, lhs_ref, 8)

    def store(g, row, lanes, values):
        x4_ref[g // 2, g % 2, row + 2, :, lanes] = values

    lift(lhs_ref, wl_ref, 8, 64, BF, store)
    for plane in range(8):
        x4_ref[plane // 2, plane % 2, 0:2] = x4b_ref[plane // 2, plane % 2, 6:8]
    conv1_rows(x4_ref, w1_ref, fn_ref, 0, 7)
    for pp in range(4):

        def row_of(a, row):
            if row < 7:
                return fnt_ref[pp, a, row]
            if row < 13:
                return fno_ref[pp, a, row - 7]
            return fn_ref[pp, a, row - 13]

        taps = [
            jnp.concatenate([row_of(a, 2 * rr + b) for rr in range(10)], axis=0)
            for a in range(2)
            for b in range(2)
        ]
        mid_ref[pp] = reduce1(taps, wr1_ref).reshape(10, 64, 128)


def outer_kernel(
    lrecv_ref, left_ref, right_ref, rrecv_ref, wl_ref, w1_ref, wr1_ref, main_ref, wr2_ref, w3_ref, c2_hbm,
    edge_ref, skip_ref, chunk_ref,
    de_ref, dw_ref, lhs_ref, x4_ref, fn_ref, me_ref, mf_ref, xm_ref, ms_ref, cf_ref, w2_ref, sem,
):
    copies = [
        pltpu.make_async_copy(
            c2_hbm, w2_ref.at[3 * q : 3 * q + 9, :, q * 128 : (q + 1) * 128], sem.at[q]
        )
        for q in range(2)
    ]
    for copy in copies:
        copy.start()
    w2_ref[0:3, :, 128:256] = jnp.zeros((3, 384, 128), BF)
    w2_ref[9:12, :, 0:128] = jnp.zeros((3, 384, 128), BF)
    de_ref[:, 0:8] = lrecv_ref[...].astype(F32)
    de_ref[:, 8:16] = left_ref[...].astype(F32)
    de_ref[:, 16:24] = right_ref[...].astype(F32)
    de_ref[:, 24:32] = rrecv_ref[...].astype(F32)
    for half in range(2):
        dw_ref[half, :, 0:8] = de_ref[:, 1 + 2 * half : 9 + 2 * half]
        dw_ref[half, :, 8:16] = de_ref[:, 21 + 2 * half : 29 + 2 * half]
    for half in range(2):
        for g in range(0, 24, 2):
            lhs_ref[half, g * 8 : (g + 2) * 8, :] = jnp.concatenate(
                [
                    jnp.concatenate(
                        [dw_ref[half, g + k, pl.ds(j, 8, stride=2)] for k in range(2)], axis=0
                    )
                    for j in range(2)
                ],
                axis=1,
            ).astype(BF)

    zero = jnp.zeros((24, 8, 256), F32)
    x4_ref[0, 1] = zero
    x4_ref[5, 0] = zero

    def store(g, row, lanes, values):
        x4_ref[1 + g % 8 // 2, g % 2, g // 8 * 8 + row, :, lanes] = values

    lift(lhs_ref, wl_ref, 24, 8, F32, store)
    out = conv1(
        lambda h, s, b: x4_ref[1 + h : 5 + h, s, 1 + b : 21 + b].reshape(640, 256),
        w1_ref,
        range(4),
    ).astype(F32)
    for q in range(2):
        fn_ref[:, q] = out[:, q * 128 : (q + 1) * 128].reshape(4, 10, 2, 8, 128)
    edge_ref[...] = fn_ref[:, :, 3:7].reshape(8, 8, 8, 128)
    taps = [fn_ref[:, a, :, b].reshape(320, 128) for a in range(2) for b in range(2)]
    me_ref[...] = reduce1(taps, wr1_ref).astype(F32).reshape(4, 10, 8, 128)

    for n in range(40):
        plane, row = n // 10, n % 10
        mf_ref[n, 16:80] = main_ref[plane, row].astype(F32)
        mf_ref[n, 13:17] = me_ref[plane, row, 0:4]
        mf_ref[n, 79:83] = me_ref[plane, row, 4:8]
        for c in range(3):
            xm_ref[plane, row, :, c * 128 : (c + 1) * 128] = mf_ref[n, 7 + c : 87 + c].astype(BF)
    for copy in copies:
        copy.wait()
    for half in range(2):
        taps = range(1, 4) if half == 0 else range(0, 3)
        lhs = jnp.concatenate(
            [
                xm_ref[2 * half - 1 + dp, b : b + 8].reshape(640, 384)
                for dp in taps
                for b in range(3)
            ],
            axis=1,
        )
        weight = w2_ref[taps[0] * 3 : taps[0] * 3 + 9].reshape(3456, 256)
        out = rounded(leaky(mm(lhs, weight)))
        for q in range(2):
            ms_ref[2 * half + q, :, 0:80] = out[:, q * 128 : (q + 1) * 128].reshape(8, 80, 128)
    for plane in range(4):
        skip_ref[plane] = ms_ref[plane, 2:6, 8:72].astype(BF)
    taps = []
    for a in range(2):
        for b in range(2):
            for c in range(2):
                taps.append(
                    jnp.concatenate(
                        [
                            ms_ref[2 * plane + a, 2 * row + b, pl.ds(6 + c, 40, stride=2)]
                            for plane in range(2)
                            for row in range(4)
                        ],
                        axis=0,
                    )
                )
    lhs = jnp.concatenate(taps, axis=1).astype(BF)
    out = rounded(leaky(mm(lhs, wr2_ref[...])))
    cf_ref[...] = out.reshape(2, 4, 40, 256)
    lhs = []
    for plane in range(2):
        lhs.append(
            jnp.concatenate(
                [
                    jnp.concatenate(
                        [cf_ref[plane, row + b, c : c + 32] for row in range(2)], axis=0
                    )
                    for b in range(3)
                    for c in range(3)
                ],
                axis=1,
            ).astype(BF)
        )
    same = mm(jnp.concatenate(lhs, axis=0), w3_ref[1])
    first = same[0:64] + mm(lhs[1], w3_ref[2])
    second = same[64:128] + mm(lhs[0], w3_ref[0])
    out = jnp.concatenate([first[0:32], second[0:32], first[32:64], second[32:64]], axis=0)
    out = leaky(out).T
    chunk_ref[...] = out.reshape(64, 4, 128).astype(BF)


def finest_kernel(fnt_ref, fno_ref, fnb_ref, edge_ref, out_ref, wide_ref, rows_ref):
    lane = lax.broadcasted_iota(jnp.int32, (64, 128), 1)
    pair = lax.broadcasted_iota(jnp.int32, (64, 128), 0)
    for row in range(0, 8, 2):
        now = []
        for r in (row, row + 1):
            v = (fnt_ref[0, 0] if r == 0 else fnb_ref[0, 0] if r == 7 else fno_ref[0, r - 1]).astype(F32)
            v = jnp.where(pair == 0, edge_ref[0, r, 3:4], v)
            now.append(jnp.where(pair == 63, edge_ref[0, r, 4:5], v))
        wide_ref[row // 2, pl.ds(0, 64, stride=2), :] = jnp.where(
            lane < 64, now[0], pltpu.roll(now[1], 64, 1)
        )
        wide_ref[row // 2, pl.ds(1, 64, stride=2), :] = jnp.where(
            lane < 64, pltpu.roll(now[0], 64, 1), now[1]
        )
        turned = wide_ref[row // 2].T
        rows_ref[:, row, :] = turned[0:64]
        rows_ref[:, row + 1, :] = turned[64:128]
    out_ref[:, 0] = rows_ref[...].astype(BF)


def coarse_kernel(in_ref, out_ref, y_ref):
    all_in = in_ref[...].astype(F32)
    for c in range(4):
        v = all_in[:, c, :]
        y_ref[c, pl.ds(0, 64, stride=2), :] = v
        y_ref[c, pl.ds(1, 64, stride=2), :] = pltpu.roll(v, 64, 1)
    for c in range(4):
        out_ref[c] = y_ref[c].T[0:64].reshape(2, 32, 128).astype(BF)


def shift(array, axis, step):
    peers = lax.axis_size(axis)
    return lax.ppermute(array, axis, [(i, (i + step) % peers) for i in range(peers)])


def struct(shape, dtype):
    return jax.ShapeDtypeStruct(shape, dtype)


def on_device(disp, lift_w, conv1_w, reduce1_w, conv2_w, reduce2_w, conv3_w):
    own = disp.reshape(24, 8, 128)
    up = shift(own, "wide", 1)
    strip = struct((8, 8, 128), F32)
    fine_scratch = (VMEM((2, 512, 256), BF), VMEM((4, 2, 10, 64, 256), BF))
    turn_scratch = (VMEM((8, 144, 128), F32),)
    stay = lambda x: pltpu.with_memory_space_constraint(x, pltpu.HBM)
    x4b, lown, rown, wl, w1 = call(
        own_kernel,
        (
            struct((4, 2, 8, 64, 256), BF),
            strip,
            strip,
            struct((4, 256, 256), BF),
            struct((12, 256, 256), BF),
        ),
        (stay(own), stay(lift_w), stay(conv1_w.reshape(9, 192, 64))),
        14,
        scratch=turn_scratch
        + (
            VMEM((2, 512, 256), BF),
            VMEM((24, 8, 128), F32),
            VMEM((3, 64), F32),
            VMEM((9, 192, 64), BF),
            pltpu.SemaphoreType.DMA((3,)),
        ),
        name="fine_own_lift",
        flops=2 * 10**9,
        nbytes=6 * 10**6,
        space=pltpu.HBM,
    )
    again, x4b = lax.optimization_barrier((own, x4b))
    down = shift(again, "wide", -1)
    fnt, lup, rup = call(
        top_kernel,
        (struct((4, 2, 7, 64, 128), BF), strip, strip),
        (up, x4b, wl, w1),
        12,
        scratch=turn_scratch + fine_scratch,
        name="fine_top_rows",
        flops=3 * 10**9,
        nbytes=6 * 10**6,
    )
    dt, left, right = call(
        turn_kernel,
        (struct((8, 144, 128), F32), struct((24, 8, 128), BF), struct((24, 8, 128), BF)),
        (down, lup, rup, lown, rown),
        6,
        name="columns_to_rows",
        flops=10**7,
        nbytes=2 * 10**6,
    )
    rrecv = shift(left, "narrow", -1)
    fno = call(
        own_rows_kernel,
        struct((4, 2, 6, 64, 128), BF),
        (x4b, w1),
        8,
        name="fine_own_rows",
        flops=2 * 10**9,
        nbytes=6 * 10**6,
    )
    again, fno = lax.optimization_barrier((right, fno))
    lrecv = shift(again, "narrow", 1)
    dt, rrecv = lax.optimization_barrier((dt, rrecv))
    wr1 = reduce1_w.reshape(512, 128)
    fnb, mid = call(
        bottom_kernel,
        (struct((4, 2, 7, 64, 128), BF), struct((4, 10, 64, 128), BF)),
        (dt, x4b, fnt, fno, wl, w1, wr1),
        14,
        scratch=fine_scratch,
        name="fine_bottom_rows",
        flops=8 * 10**9,
        nbytes=6 * 10**6,
    )
    edge, skip, chunk = call(
        outer_kernel,
        (struct((8, 8, 8, 128), F32), struct((4, 4, 64, 128), BF), struct((64, 4, 128), BF)),
        (
            lrecv, left, right, rrecv, wl, w1, wr1, mid,
            reduce2_w.reshape(1024, 256), conv3_w.reshape(3, 2304, 256),
            stay(conv2_w.reshape(9, 384, 128)),
        ),
        26,
        last=pltpu.HBM,
        scratch=(
            VMEM((24, 32, 128), F32),
            VMEM((2, 24, 16, 128), F32),
            VMEM((2, 192, 256), BF),
            VMEM((6, 2, 24, 8, 256), F32),
            VMEM((4, 2, 10, 2, 8, 128), F32),
            VMEM((4, 10, 8, 128), F32),
            VMEM((40, 96, 128), F32),
            VMEM((4, 10, 80, 384), BF),
            VMEM((4, 8, 88, 128), F32),
            VMEM((2, 4, 40, 256), F32),
            VMEM((12, 384, 256), BF),
            pltpu.SemaphoreType.DMA((2,)),
        ),
        name="middle_and_coarse",
        flops=6 * 10**9,
        nbytes=12 * 10**6,
    )
    received = lax.all_to_all(chunk, "wide", 0, 0, tiled=True)
    finest = pl.pallas_call(
        finest_kernel,
        grid=(8,),
        out_shape=struct((64, 8, 8, 128), BF),
        in_specs=[
            pl.BlockSpec((1, 1, 64, 128), lambda p: (p, 6, 0, 0)),
            pl.BlockSpec((1, 6, 64, 128), lambda p: (p, 0, 0, 0)),
            pl.BlockSpec((1, 1, 64, 128), lambda p: (p, 0, 0, 0)),
            pl.BlockSpec((1, 8, 8, 128), lambda p: (p, 0, 0, 0)),
        ],
        out_specs=pl.BlockSpec((64, 1, 8, 128), lambda p: (0, p, 0, 0)),
        scratch_shapes=[VMEM((4, 128, 128), F32), VMEM((64, 8, 128), F32)],
        compiler_params=pltpu.CompilerParams(vmem_limit_bytes=6 * MIB),
        cost_estimate=pl.CostEstimate(flops=10**8, bytes_accessed=3 * 10**6, transcendentals=0),
        name="finest_layout",
    )(
        fnt.reshape(8, 7, 64, 128),
        fno.reshape(8, 6, 64, 128),
        fnb.reshape(8, 7, 64, 128),
        edge,
    )
    coarse = call(
        coarse_kernel,
        struct((4, 2, 32, 128), BF),
        (received,),
        4,
        scratch=(VMEM((4, 128, 128), F32),),
        name="coarse_layout",
        flops=10**6,
        nbytes=2 * 10**5,
    )
    return finest, skip.transpose(3, 0, 1, 2), coarse.transpose(0, 1, 3, 2)


def solution(mesh):
    return jax.shard_map(
        on_device,
        mesh=mesh,
        in_specs=(P(None, None, "wide", "narrow"), P(), P(), P(), P(), P(), P()),
        out_specs=(
            P(None, None, "wide", "narrow"),
            P(None, None, "wide", "narrow"),
            P("wide", None, None, "narrow"),
        ),
        check_vma=False,
    )
```
